128 devices in a mesh: mesh: 32 (over y, x, core), state: 4 (over z).
Axes of the slice: x: 4, y: 4, z: 4, core: 2. Of those that a mesh axis runs over, the one named last changes fastest.
Arguments:
- kern_blocks: bfloat16 [768, 16, 128, 128], P('mesh'), may hold values from 4.296875e-06 to 0.13744531
- kern_cols: int32 [768, 16], P('mesh'), may hold values from 0 to 767, as said below
- state_kernel: bfloat16 [512, 512], replicated, may hold values from 0 to 0.61, as said below
- start_v: float32 [98304, 512], P('mesh', 'state'), may hold values from 0.5 to 5
- mu: float32 [98304, 512], P(('mesh', 'state')), may hold values from 0.2 to 2
- nu: float32 [98304, 512], P('mesh', 'state'), may hold values from 0.2 to 2
Outputs:
- potential_u: float32 [98304, 512], P(('mesh', 'state'))
- potential_v: float32 [98304, 512], P('mesh', 'state')
The draws below stay inside these ranges and needn't reach their ends.
Inputs may be any that keep to these rules, and one draw needn't show every extreme that they name: `kern_cols`: each block row names 16 different block columns, its own block among them. The block rows held by index d of mesh (rows d * 24 to (d + 1) * 24 - 1) refer, among the blocks of index d - 1 and d + 1 (wrapping around 32), only to the last 6 blocks of d - 1 and the first 6 blocks of d + 1, and to all of them; among the blocks of every other index, to at most 2 distinct blocks, and to exactly 2 of index d + 2. How many other indices they reach differs from index to index. `state_kernel`: each row has a positive diagonal entry.
All inputs are finite; a program needn't handle non-finite values.
Results may differ from the reference program's by a relative error of at most 0.0033.
Values may be sent and summed in bfloat16 or wider, within the bound.
A program may use at most 192 MiB of HBM per device.

```python
import math
import jax
import jax.numpy as jnp
from jax import lax

B = 128
DEG = 16
N2 = 512
NBR_DEV = 24
CAP_FAR = 2
ITERS = 2
CAP_NEAR = 6
NB = 768
N1 = 98304
N_MESH = 32


def draw_kern_blocks(key, part):
    key_back = jax.random.fold_in(key, 21)
    key_peak = jax.random.fold_in(key, 22)
    key_gain = jax.random.fold_in(key, 23)
    key_shift = jax.random.fold_in(key, 24)
    row_ids = jnp.arange(B, dtype=jnp.int32)[:, None]
    col_ids = jnp.arange(B, dtype=jnp.int32)[None, :]
    offset = jax.random.randint(key_shift, (NB, DEG, 1, 1), 0, B, dtype=jnp.int32)
    on_peak = col_ids[None, None] == (row_ids[None, None] + offset) % B
    back_draw = jax.random.uniform(key_back, (NB, DEG, B, B), jnp.float32)
    peak_draw = jax.random.uniform(key_peak, (NB, DEG, B, 1), jnp.float32)
    gain_draw = jax.random.uniform(key_gain, (NB, DEG, 1, 1), jnp.float32)
    background = 0.2 * jnp.exp(back_draw * math.log(8.0)) / B
    peak_value = jnp.exp(peak_draw * math.log(3.0))
    gain_value = 0.045 * jnp.exp(gain_draw * math.log(16.0)) / DEG
    entries = gain_value * (background + jnp.where(on_peak, peak_value, 0.0))
    return entries.astype(jnp.bfloat16)


def draw_state_kernel(key, part):
    key_order = jax.random.fold_in(key, 31)
    key_factor = jax.random.fold_in(key, 32)
    position = jax.random.permutation(key_order, N2).astype(jnp.int32)
    spacing = jnp.abs(position[:, None] - position[None, :])
    cycle_gap = jnp.minimum(spacing, N2 - spacing).astype(jnp.float32)
    profile = jnp.exp(-cycle_gap * cycle_gap / 4.0)
    factor_draw = jax.random.uniform(key_factor, (N2, N2), jnp.float32)
    factor = 0.25 * jnp.exp(factor_draw * math.log(16.0))
    return (0.15 * factor * profile).astype(jnp.bfloat16)


def draw_kern_cols(key, part):
    peer_count = NB // NBR_DEV
    far_count = peer_count - 3
    pool_size = NBR_DEV + 2 * CAP_NEAR + far_count * CAP_FAR
    devices = jnp.arange(peer_count, dtype=jnp.int32)
    local_ids = devices[:, None] * NBR_DEV + jnp.arange(NBR_DEV, dtype=jnp.int32)[None, :]
    left_ids = ((devices + peer_count - 1) % peer_count)[:, None] * NBR_DEV + (NBR_DEV - CAP_NEAR + jnp.arange(CAP_NEAR, dtype=jnp.int32))[None, :]
    right_ids = ((devices + 1) % peer_count)[:, None] * NBR_DEV + jnp.arange(CAP_NEAR, dtype=jnp.int32)[None, :]
    far_peer = (devices[:, None] + 2 + jnp.arange(far_count, dtype=jnp.int32)[None, :]) % peer_count
    key_first = jax.random.fold_in(key, 11)
    key_step = jax.random.fold_in(key, 12)
    key_count = jax.random.fold_in(key, 13)
    key_score = jax.random.fold_in(key, 14)
    first = jax.random.randint(key_first, (peer_count, far_count), 0, NBR_DEV, dtype=jnp.int32)
    stride = jax.random.randint(key_step, (peer_count, far_count), 1, NBR_DEV, dtype=jnp.int32)
    far_local = (first[:, :, None] + jnp.arange(CAP_FAR, dtype=jnp.int32)[None, None, :] * stride[:, :, None]) % NBR_DEV
    far_ids = (far_peer[:, :, None] * NBR_DEV + far_local).reshape(peer_count, far_count * CAP_FAR)
    candidates = jnp.concatenate([local_ids, left_ids, right_ids, far_ids], axis=1)
    in_use = jax.random.randint(key_count, (peer_count,), 1, far_count + 1, dtype=jnp.int32)
    extra_count = 2 * CAP_NEAR + far_count * CAP_FAR
    extra_pos = jnp.arange(extra_count, dtype=jnp.int32)
    far_order = jnp.maximum(extra_pos - 2 * CAP_NEAR, 0) // CAP_FAR
    extra_active = (extra_pos < 2 * CAP_NEAR)[None, :] | (far_order[None, :] < in_use[:, None])
    extra_row = extra_pos % NBR_DEV
    row_ids = jnp.arange(NBR_DEV, dtype=jnp.int32)
    local_forced = (row_ids[:, None] == row_ids[None, :]).astype(jnp.int32)
    extra_forced = (row_ids[None, :, None] == extra_row[None, None, :]) & extra_active[:, None, :]
    forced = jnp.concatenate([jnp.broadcast_to(local_forced[None], (peer_count, NBR_DEV, NBR_DEV)), extra_forced.astype(jnp.int32)], axis=2)
    active = jnp.concatenate([jnp.ones((peer_count, NBR_DEV), jnp.int32), extra_active.astype(jnp.int32)], axis=1)
    level = jnp.where(forced > 0, 3, jnp.broadcast_to(active[:, None, :], forced.shape))
    noise = jax.random.randint(key_score, (peer_count, NBR_DEV, pool_size), 0, 4096, dtype=jnp.int32)
    scores = level * 1048576 + noise * pool_size + jnp.arange(pool_size, dtype=jnp.int32)[None, None, :]
    _, picked = lax.top_k(scores, DEG)
    chosen = jnp.take_along_axis(jnp.broadcast_to(candidates[:, None, :], scores.shape), picked, axis=2)
    return chosen.reshape(NB, DEG).astype(jnp.int32)


def steps_of(key, shape, split, least, largest):
    def one(dim, shards_of):
        heights = jax.random.uniform(jax.random.fold_in(jax.random.fold_in(key, 6), dim), (shards_of,), jnp.float32, least / len(split), largest / len(split))
        return jnp.repeat(jnp.exp(heights), shape[dim] // shards_of).reshape((-1,) + (1,) * (len(shape) - dim - 1))

    level = one(*split[0])
    for cut in split[1:]:
        level = level * one(*cut)
    return level


def setup_inputs(seed: int = 0) -> dict:
    streams_of = jax.random.split(jax.random.key(seed), 7)
    kern_blocks = draw_kern_blocks(jax.random.fold_in(streams_of[6], 71), 0)
    kern_cols = draw_kern_cols(jax.random.fold_in(streams_of[6], 71), 0)
    state_kernel = draw_state_kernel(jax.random.fold_in(streams_of[6], 71), 0)
    start_v = jnp.clip(jnp.exp(math.log(5.0) - 2.3025851 * jax.random.uniform(streams_of[3], (N1, N2), jnp.float32) ** steps_of(streams_of[3], (N1, N2), ((0, 32), (1, 4)), -0.2, 0.2)), 0.5, 5.0)
    mu = jnp.clip(jnp.exp(math.log(2.0) - 2.3025851 * jax.random.uniform(streams_of[4], (N1, N2), jnp.float32) ** steps_of(streams_of[4], (N1, N2), ((0, 128),), -0.2, 0.2)), 0.2, 2.0)
    nu = jnp.clip(jnp.exp(math.log(2.0) - 2.3025851 * jax.random.uniform(streams_of[5], (N1, N2), jnp.float32) ** steps_of(streams_of[5], (N1, N2), ((0, 32), (1, 4)), -0.2, 0.2)), 0.2, 2.0)
    return dict(kern_blocks=kern_blocks, kern_cols=kern_cols, state_kernel=state_kernel, start_v=start_v, mu=mu, nu=nu)


def forward_mesh(kern_blocks, kern_cols, rounded_v):
    blocks = rounded_v.reshape(NB, B, N2)

    def one_row(pair):
        kern_row, col_row = pair
        picked = blocks[col_row].astype(jnp.float32)
        return jnp.einsum("kab,kbc->ac", kern_row.astype(jnp.float32), picked)

    return lax.map(one_row, (kern_blocks, kern_cols)).reshape(NB * B, N2)


def backward_mesh(kern_blocks, kern_cols, rounded_b):
    kern_dev = kern_blocks.reshape(N_MESH, NBR_DEV, DEG, B, B)
    cols_dev = kern_cols.reshape(N_MESH, NBR_DEV * DEG)
    rows_dev = rounded_b.reshape(N_MESH, NBR_DEV, B, N2)

    def add_device(total, triple):
        kern_part, col_part, row_part = triple
        spread = jnp.einsum("rkab,rac->rkbc", kern_part.astype(jnp.float32), row_part.astype(jnp.float32))
        partial_value = jax.ops.segment_sum(spread.reshape(NBR_DEV * DEG, B, N2), col_part, num_segments=NB)
        partial_value = lax.optimization_barrier(partial_value.astype(jnp.bfloat16)).astype(jnp.float32)
        return total + partial_value, None

    start = jnp.zeros((NB, B, N2), jnp.float32)
    total, _ = lax.scan(add_device, start, (kern_dev, cols_dev, rows_dev))
    return total.reshape(NB * B, N2)


def reference(kern_blocks, kern_cols, state_kernel, start_v, mu, nu):
    values = start_v
    potential_u = mu
    for sweep in range(ITERS):
        rounded_v = lax.optimization_barrier(values.astype(jnp.bfloat16))
        applied = forward_mesh(kern_blocks, kern_cols, rounded_v).astype(jnp.bfloat16)
        mixed = jnp.dot(applied, state_kernel.T, preferred_element_type=jnp.float32)
        potential_u = mu / mixed
        back_rows = jnp.dot(potential_u.astype(jnp.bfloat16), state_kernel, preferred_element_type=jnp.float32).astype(jnp.bfloat16)
        rounded_b = lax.optimization_barrier(back_rows)
        totals = backward_mesh(kern_blocks, kern_cols, rounded_b)
        values = nu / totals
    return potential_u, values
```

```python
import functools
import jax
import jax.numpy as jnp
from jax import lax
from jax.experimental import pallas as pl
from jax.experimental.pallas import tpu as pltpu
from jax.sharding import PartitionSpec as P

ITERS = 2
NEAR = 6
FAR = 2
VMEM_LIMIT = 48 * 1024 * 1024
F32 = jnp.float32
BF16 = jnp.bfloat16


def vmem():
    return pl.BlockSpec(memory_space=pltpu.VMEM)


def smem():
    return pl.BlockSpec(memory_space=pltpu.SMEM)


def far_plan(flat_cols, me, peers, rows):
    owners = flat_cols // rows
    places = flat_cols % rows
    delta = (owners - me + peers) % peers
    is_own = delta == 0
    is_left = delta == peers - 1
    is_right = delta == 1
    is_far = ~(is_own | is_left | is_right)
    ids = jnp.arange(peers * rows, dtype=jnp.int32)
    hits = (flat_cols[:, None] == ids[None, :]) & is_far[:, None]
    needed = jnp.max(hits.astype(jnp.int32), axis=0).reshape(peers, rows)
    before = jnp.arange(rows)[:, None] < jnp.arange(rows)[None, :]
    ranks = jnp.sum(needed[:, :, None] * before[None].astype(jnp.int32), axis=1)
    place_ids = jnp.arange(rows, dtype=jnp.int32)
    requests = jnp.stack(
        [jnp.sum(needed * (ranks == s) * place_ids[None, :], axis=1) for s in range(FAR)],
        axis=1,
    )
    slots = jnp.sum(hits.astype(jnp.int32) * ranks.reshape(1, -1), axis=1)
    sources = jnp.where(
        is_own,
        places,
        jnp.where(
            is_left,
            rows + places - (rows - NEAR),
            jnp.where(is_right, rows + NEAR + places, rows + 2 * NEAR + owners * FAR + slots),
        ),
    )
    return sources.astype(jnp.int32), requests.astype(jnp.int32)


def prep_kernel(asked_ref, v_ref, blocks_ref, send_ref):
    def cast(i, _):
        blocks_ref[i] = v_ref[i].astype(BF16)
        return 0

    lax.fori_loop(0, v_ref.shape[0], cast, 0)

    def pick(e, _):
        send_ref[e] = blocks_ref[asked_ref[e]]
        return 0

    lax.fori_loop(0, send_ref.shape[0], pick, 0)


def forward_kernel(src_ref, kern_ref, own_ref, left_ref, right_ref, far_ref, out_ref, table, sems):
    r = pl.program_id(0)
    rows = own_ref.shape[0]

    @pl.when(r == 0)
    def _():
        copies = [
            pltpu.make_async_copy(own_ref, table.at[pl.ds(0, rows)], sems.at[0]),
            pltpu.make_async_copy(left_ref, table.at[pl.ds(rows, NEAR)], sems.at[1]),
            pltpu.make_async_copy(right_ref, table.at[pl.ds(rows + NEAR, NEAR)], sems.at[2]),
            pltpu.make_async_copy(
                far_ref, table.at[pl.ds(rows + 2 * NEAR, far_ref.shape[0])], sems.at[3]
            ),
        ]
        for c in copies:
            c.start()
        for c in copies:
            c.wait()

    degree = kern_ref.shape[1]
    lhs = jnp.concatenate([kern_ref[0, k] for k in range(degree)], axis=1)
    rhs = jnp.concatenate([table[src_ref[r * degree + k]] for k in range(degree)], axis=0)
    out_ref[0] = jnp.dot(lhs, rhs, preferred_element_type=F32).astype(BF16)


def backward_kernel(src_ref, kern_ref, b_ref, own_ref, left_ref, right_ref, far_ref, acc):
    r = pl.program_id(0)
    rows = own_ref.shape[0]
    degree = kern_ref.shape[1]
    size = b_ref.shape[1]

    @pl.when(r == 0)
    def _():
        def clear(i, _):
            acc[i] = jnp.zeros(acc.shape[1:], F32)
            return 0

        lax.fori_loop(0, acc.shape[0], clear, 0)

    b_t = b_ref[0].T
    for k in range(0, degree, 2):
        rhs = jnp.concatenate([kern_ref[0, k], kern_ref[0, k + 1]], axis=1)
        prod = jnp.dot(b_t, rhs, preferred_element_type=F32)
        acc[src_ref[r * degree + k]] += prod[:, :size]
        acc[src_ref[r * degree + k + 1]] += prod[:, size:]

    @pl.when(r == pl.num_programs(0) - 1)
    def _():
        def store(ref, base):
            def body(i, _):
                ref[i] = acc[base + i].T.astype(BF16)
                return 0

            lax.fori_loop(0, ref.shape[0], body, 0)

        store(own_ref, 0)
        store(left_ref, rows)
        store(right_ref, rows + NEAR)
        store(far_ref, rows + 2 * NEAR)


def finish_kernel(
    last, asked_ref, own_ref, first_ref, last_ref, far_ref, nu_ref, *rest
):
    if last:
        v_ref, acc = rest
    else:
        blocks_ref, send_ref, acc = rest
    rows = own_ref.shape[0]

    def start(i, _):
        acc[i] = own_ref[i].astype(F32)
        return 0

    lax.fori_loop(0, rows, start, 0)

    def near(i, _):
        acc[i] += first_ref[i].astype(F32)
        j = rows - NEAR + i
        acc[j] += last_ref[i].astype(F32)
        return 0

    lax.fori_loop(0, NEAR, near, 0)

    def far(e, _):
        acc[asked_ref[e]] += far_ref[e].astype(F32)
        return 0

    lax.fori_loop(0, far_ref.shape[0], far, 0)

    def divide(i, _):
        v = nu_ref[i] / acc[i]
        if last:
            v_ref[i] = v
        else:
            blocks_ref[i] = v.astype(BF16)
        return 0

    lax.fori_loop(0, rows, divide, 0)
    if not last:

        def pick(e, _):
            send_ref[e] = blocks_ref[asked_ref[e]]
            return 0

        lax.fori_loop(0, send_ref.shape[0], pick, 0)


def params():
    return pltpu.CompilerParams(vmem_limit_bytes=VMEM_LIMIT)


def per_device(kern_blocks, kern_cols, state_kernel, start_v, mu, nu):
    rows, degree, size, _ = kern_blocks.shape
    local_rows, cols = start_v.shape
    peers = lax.axis_size("mesh")
    states = lax.axis_size("state")
    me = lax.axis_index("mesh")
    nfar = peers * FAR
    table_size = rows + 2 * NEAR + nfar
    sources, requests = far_plan(kern_cols.reshape(-1), me, peers, rows)
    asked = lax.all_to_all(requests, "mesh", split_axis=0, concat_axis=0, tiled=True).reshape(-1)

    def blk(n, dtype=BF16):
        return jax.ShapeDtypeStruct((n, size, cols), dtype)

    up = [(i, (i + 1) % peers) for i in range(peers)]
    down = [(i, (i + peers - 1) % peers) for i in range(peers)]

    def swap_far(x):
        return lax.all_to_all(x, "mesh", split_axis=0, concat_axis=0, tiled=True)

    blocks, send = pl.pallas_call(
        prep_kernel,
        out_shape=(blk(rows), blk(nfar)),
        in_specs=[smem(), vmem()],
        out_specs=(vmem(), vmem()),
        compiler_params=params(),
        name="prep",
    )(asked, start_v.reshape(rows, size, cols))

    nu_blocks = nu.reshape(rows, size, cols)
    kern_spec = pl.BlockSpec((1, degree, size, size), lambda r, s: (r, 0, 0, 0))
    row_spec = pl.BlockSpec((1, size, cols), lambda r, s: (r, 0, 0))
    any_spec = pl.BlockSpec(memory_space=pl.ANY)

    def whole(n):
        return pl.BlockSpec((n, size, cols), lambda r, s: (0, 0, 0))

    potential_u = mu
    values = None
    for sweep in range(ITERS):
        from_left = lax.ppermute(blocks[rows - NEAR :], "mesh", up)
        from_right = lax.ppermute(blocks[:NEAR], "mesh", down)
        far = swap_far(send)
        applied = pl.pallas_call(
            forward_kernel,
            grid_spec=pltpu.PrefetchScalarGridSpec(
                num_scalar_prefetch=1,
                grid=(rows,),
                in_specs=[kern_spec, any_spec, any_spec, any_spec, any_spec],
                out_specs=row_spec,
                scratch_shapes=[
                    pltpu.VMEM((table_size, size, cols), BF16),
                    pltpu.SemaphoreType.DMA((4,)),
                ],
            ),
            out_shape=blk(rows),
            compiler_params=params(),
            name="forward",
        )(sources, kern_blocks, blocks, from_left, from_right, far)
        pieces = applied.reshape(states, local_rows // states, cols)
        mixed = jnp.einsum(
            "xrl,jl->xrj",
            lax.all_to_all(pieces, "state", split_axis=0, concat_axis=2, tiled=True),
            state_kernel,
            preferred_element_type=F32,
        )
        potential_u = mu / mixed[0]
        back_rows = jnp.dot(
            potential_u.astype(BF16), state_kernel, preferred_element_type=F32
        ).astype(BF16)
        returned = lax.all_to_all(back_rows, "state", split_axis=1, concat_axis=0, tiled=True)
        returned = returned.reshape(rows, size, cols)
        own, to_left, to_right, to_far = pl.pallas_call(
            backward_kernel,
            grid_spec=pltpu.PrefetchScalarGridSpec(
                num_scalar_prefetch=1,
                grid=(rows,),
                in_specs=[kern_spec, row_spec],
                out_specs=(whole(rows), whole(NEAR), whole(NEAR), whole(nfar)),
                scratch_shapes=[pltpu.VMEM((table_size, size, cols), F32)],
            ),
            out_shape=(blk(rows), blk(NEAR), blk(NEAR), blk(nfar)),
            compiler_params=params(),
            name="backward",
        )(sources, kern_blocks, returned)
        part_last = lax.ppermute(to_left, "mesh", down)
        part_first = lax.ppermute(to_right, "mesh", up)
        part_far = swap_far(to_far)
        last = sweep == ITERS - 1
        result = pl.pallas_call(
            functools.partial(finish_kernel, last),
            out_shape=(blk(rows, F32),) if last else (blk(rows), blk(nfar)),
            in_specs=[smem()] + [vmem()] * 5,
            out_specs=(vmem(),) if last else (vmem(), vmem()),
            scratch_shapes=[pltpu.VMEM((rows, size, cols), F32)],
            compiler_params=params(),
            name="finish",
        )(asked, own, part_first, part_last, part_far, nu_blocks)
        if last:
            values = result[0]
        else:
            blocks, send = result
    return (potential_u, values.reshape(local_rows, cols))


def solution(mesh):
    placed = (
        P("mesh", None, None, None),
        P("mesh", None),
        P(),
        P("mesh", "state"),
        P(("mesh", "state"), None),
        P("mesh", "state"),
    )
    return jax.shard_map(
        per_device,
        mesh=mesh,
        in_specs=placed,
        out_specs=(P(("mesh", "state"), None), P("mesh", "state")),
        check_vma=False,
    )
```

```python
import functools
import jax
import jax.numpy as jnp
from jax import lax
from jax.experimental import pallas as pl
from jax.experimental.pallas import tpu as pltpu
from jax.sharding import PartitionSpec as P

ITERS = 2
NEAR = 6
FAR = 2
LAG = 2
VMEM_LIMIT = 52 * 1024 * 1024
F32 = jnp.float32
BF16 = jnp.bfloat16


def vmem():
    return pl.BlockSpec(memory_space=pltpu.VMEM)


def smem():
    return pl.BlockSpec(memory_space=pltpu.SMEM)


def hbm():
    return pl.BlockSpec(memory_space=pl.ANY)


def far_plan(flat_cols, me, peers, rows):
    owners = flat_cols // rows
    places = flat_cols % rows
    delta = (owners - me + peers) % peers
    is_own = delta == 0
    is_left = delta == peers - 1
    is_right = delta == 1
    is_far = ~(is_own | is_left | is_right)
    ids = jnp.arange(peers * rows, dtype=jnp.int32)
    hits = (flat_cols[:, None] == ids[None, :]) & is_far[:, None]
    needed = jnp.max(hits.astype(jnp.int32), axis=0).reshape(peers, rows)
    before = jnp.arange(rows)[:, None] < jnp.arange(rows)[None, :]
    ranks = jnp.sum(needed[:, :, None] * before[None].astype(jnp.int32), axis=1)
    place_ids = jnp.arange(rows, dtype=jnp.int32)
    requests = jnp.stack(
        [jnp.sum(needed * (ranks == s) * place_ids[None, :], axis=1) for s in range(FAR)],
        axis=1,
    )
    slots = jnp.sum(hits.astype(jnp.int32) * ranks.reshape(1, -1), axis=1)
    far_at = rows + 2 * NEAR + (delta - 2) * FAR + slots
    sources = jnp.where(
        is_own,
        places,
        jnp.where(
            is_left,
            rows + places - (rows - NEAR),
            jnp.where(is_right, rows + NEAR + places, far_at),
        ),
    )
    return sources.astype(jnp.int32), requests.astype(jnp.int32)


def arrival_order(asked, me, peers, rows):
    deltas = (me + jnp.arange(2, peers - 1, dtype=jnp.int32)) % peers
    places = asked.reshape(peers, FAR)[deltas].reshape(-1)
    count = places.shape[0]
    ids = jnp.arange(count, dtype=jnp.int32)
    keys = places * count + ids
    rank = jnp.sum((keys[None, :] < keys[:, None]).astype(jnp.int32), axis=1)
    here = (rank[:, None] == ids[None, :]).astype(jnp.int32)
    perm = jnp.sum(here * ids[:, None], axis=0)
    ordered = jnp.sum(here * places[:, None], axis=0)
    keep = jnp.concatenate([jnp.zeros((1,), jnp.int32), (ordered[1:] == ordered[:-1]).astype(jnp.int32)])
    same = ordered[None, :] == jnp.arange(rows, dtype=jnp.int32)[:, None]
    last = jnp.max(jnp.where(same, ids[None, :], -1), axis=1)
    return perm, keep, last


def exchange_kernel(mode, with_u, peers, states, *refs):
    with_back = mode != "first"
    with_forward = mode != "last"
    refs = list(refs)

    def take(n):
        out = refs[:n]
        del refs[:n]
        return out

    if with_back:
        perm_ref, keep_ref, last_ref, parts_ref, nu_hbm = take(5)
    else:
        (start_ref,) = take(1)
    if with_forward:
        asked_ref, src_ref, kern_hbm, mix_hbm, mu_hbm = take(5)
        (back_ref,) = take(1)
        if with_u:
            (u_ref,) = take(1)
    else:
        (v_ref,) = take(1)
    if with_back:
        own_part, arrived, running, nu_ref, back_send, back_recv, local_sem = take(7)
    if with_forward:
        (
            table, blocks, outbox, kern, mix, mu_ref, a_out, a_in, b_out, b_in,
            kern_sem, mix_sem, mu_sem, near_send, near_recv, far_send, far_recv,
            a_send, a_recv, b_send, b_recv,
        ) = take(21)

    me = lax.axis_index("mesh")
    mz = lax.axis_index("state")
    nfar = peers - 3

    if with_back:
        rows = own_part.shape[0]
    else:
        rows = start_ref.shape[0]
    far0 = rows + 2 * NEAR
    per = rows // states

    local = []
    if with_back:
        local.append(pltpu.make_async_copy(parts_ref.at[pl.ds(0, rows)], own_part, local_sem.at[0]))
        local.append(pltpu.make_async_copy(nu_hbm, nu_ref, local_sem.at[1]))
    for c in local:
        c.start()
    if with_forward:
        kern_copy = pltpu.make_async_copy(kern_hbm, kern, kern_sem)
        mix_copy = pltpu.make_async_copy(mix_hbm, mix, mix_sem)
        mu_copy = pltpu.make_async_copy(mu_hbm, mu_ref, mu_sem)
        kern_copy.start()
        mix_copy.start()
        mu_copy.start()

    barrier = pltpu.get_barrier_semaphore()

    def greet(o, _):
        pl.semaphore_signal(barrier, inc=1, device_id={"mesh": lax.rem(me + o, peers)})
        return 0

    lax.fori_loop(1, peers, greet, 0)
    greeted = peers - 1
    if with_forward:
        for j in range(1, states):
            pl.semaphore_signal(barrier, inc=1, device_id={"state": lax.rem(mz + j, states)})
        greeted += states - 1
    pl.semaphore_wait(barrier, greeted)

    right = lax.rem(me + 1, peers)
    left = lax.rem(me + peers - 1, peers)

    if with_back:

        def back_far(d):
            at = peers - d
            return pltpu.make_async_remote_copy(
                src_ref=parts_ref.at[pl.ds(far0 + (d - 2) * FAR, FAR)],
                dst_ref=arrived.at[pl.ds(2 * NEAR + (at - 2) * FAR, FAR)],
                send_sem=back_send.at[d],
                recv_sem=back_recv.at[at],
                device_id={"mesh": lax.rem(me + d, peers)},
            )

        def back_near(k):
            return pltpu.make_async_remote_copy(
                src_ref=parts_ref.at[pl.ds(rows + k * NEAR, NEAR)],
                dst_ref=arrived.at[pl.ds(k * NEAR, NEAR)],
                send_sem=back_send.at[k],
                recv_sem=back_recv.at[k],
                device_id={"mesh": (left, right)[k]},
            )

        def go(d, _):
            back_far(d).start()
            return 0

        lax.fori_loop(2, peers - 1, go, 0)
        for k in range(2):
            back_near(k).start()
        for c in local:
            c.wait()

        def got(d, _):
            back_far(peers - d).wait_recv()
            return 0

        for k in range(2):
            back_near(k).wait_recv()
        lax.fori_loop(2, peers - 1, got, 0)

        def add(i, acc):
            kept = jnp.where(keep_ref[i] > 0, acc, jnp.zeros_like(acc))
            acc = kept + arrived[2 * NEAR + perm_ref[i]].astype(F32)
            running[i] = acc
            return acc

        lax.fori_loop(0, nfar * FAR, add, jnp.zeros(running.shape[1:], F32))

        def finish(p, near):
            at = last_ref[p]
            total = own_part[p].astype(F32)
            if near is not None:
                total = total + arrived[near].astype(F32)
            far = running[jnp.maximum(at, 0)]
            total = total + jnp.where(at >= 0, far, jnp.zeros_like(far))
            v = nu_ref[p] / total
            if with_forward:
                table[p] = v.astype(BF16)
                blocks[p] = v.astype(BF16)
            else:
                v_ref[p] = v
            return 0

        lax.fori_loop(0, NEAR, lambda p, _: finish(p, NEAR + p), 0)
        lax.fori_loop(NEAR, rows - NEAR, lambda p, _: finish(p, None), 0)
        lax.fori_loop(rows - NEAR, rows, lambda p, _: finish(p, p - (rows - NEAR)), 0)
    else:

        def cast(p, _):
            v = start_ref[p].astype(BF16)
            table[p] = v
            blocks[p] = v
            return 0

        lax.fori_loop(0, rows, cast, 0)

    if with_forward:

        def fwd_near(k):
            return pltpu.make_async_remote_copy(
                src_ref=blocks.at[pl.ds((rows - NEAR, 0)[k], NEAR)],
                dst_ref=table.at[pl.ds(rows + k * NEAR, NEAR)],
                send_sem=near_send.at[k],
                recv_sem=near_recv.at[k],
                device_id={"mesh": (right, left)[k]},
            )

        def fwd_far(o):
            at = peers - o
            return pltpu.make_async_remote_copy(
                src_ref=outbox.at[pl.ds(o * FAR, FAR)],
                dst_ref=table.at[pl.ds(far0 + (at - 2) * FAR, FAR)],
                send_sem=far_send.at[o],
                recv_sem=far_recv.at[at],
                device_id={"mesh": lax.rem(me + o, peers)},
            )

        def send(o, _):
            q = lax.rem(me + o, peers)
            for s in range(FAR):
                outbox[o * FAR + s] = blocks[asked_ref[q * FAR + s]]
            fwd_far(o).start()
            return 0

        lax.fori_loop(2, peers - 1, send, 0)
        for k in range(2):
            fwd_near(k).start()
        for k in range(2):
            fwd_near(k).wait_recv()

        def got_far(d, _):
            fwd_far(peers - d).wait_recv()
            return 0

        lax.fori_loop(2, peers - 1, got_far, 0)
        kern_copy.wait()
        mix_copy.wait()
        mu_copy.wait()
        degree = kern.shape[1]
        size, cols = table.shape[1:]

        def a_copy(j, sub):
            to = lax.rem(mz + j, states)
            return pltpu.make_async_remote_copy(
                src_ref=a_out.at[to, sub],
                dst_ref=a_in.at[mz, sub],
                send_sem=a_send.at[j, sub],
                recv_sem=a_recv.at[j, sub],
                device_id={"state": to},
            )

        def b_copy(j, sub):
            to = lax.rem(mz + j, states)
            return pltpu.make_async_remote_copy(
                src_ref=b_out.at[to, sub],
                dst_ref=b_in.at[mz, sub],
                send_sem=b_send.at[j, sub],
                recv_sem=b_recv.at[j, sub],
                device_id={"state": to},
            )

        def apply_rows(sub):
            for j in list(range(1, states)) + [0]:
                to = lax.rem(mz + j, states)
                r = to * per + sub
                lhs = jnp.concatenate([kern[r, k] for k in range(degree)], axis=1)
                rhs = jnp.concatenate(
                    [table[src_ref[r * degree + k]] for k in range(degree)], axis=0
                )
                out = jnp.dot(lhs, rhs, preferred_element_type=F32).astype(BF16)
                if j == 0:
                    a_in[mz, sub] = out
                else:
                    a_out[to, sub] = out
                    a_copy(j, sub).start()

        def mix_rows(sub):
            for j in range(1, states):
                a_copy(j, sub).wait_recv()
            a = jnp.concatenate([a_in[z, sub] for z in range(states)], axis=1)
            kv = lax.dot_general(
                a, mix[...], (((1,), (1,)), ((), ())), preferred_element_type=F32
            )
            at = pl.ds(pl.multiple_of(sub * size, size), size)
            u = mu_ref[at, :] / kv
            if with_u:
                u_ref[at, :] = u
            b = jnp.dot(u.astype(BF16), mix[...], preferred_element_type=F32).astype(BF16)
            for z in range(states):
                b_out[z, sub] = b[:, z * cols : (z + 1) * cols]
            for j in range(1, states):
                b_copy(j, sub).start()

        def step(sub, _):
            apply_rows(sub)

            @pl.when(sub >= LAG)
            def _():
                mix_rows(sub - LAG)

            return 0

        lax.fori_loop(0, per, step, 0)
        lax.fori_loop(per - LAG, per, lambda sub, _: (mix_rows(sub), 0)[1], 0)

        def collect(sub, _):
            for j in range(1, states):
                b_copy(j, sub).wait_recv()
                z = lax.rem(mz + states - j, states)
                back_ref[z * per + sub] = b_in[z, sub]
            back_ref[mz * per + sub] = b_out[mz, sub]
            for j in range(1, states):
                a_copy(j, sub).wait_send()
                b_copy(j, sub).wait_send()
            return 0

        lax.fori_loop(0, per, collect, 0)
        for k in range(2):
            fwd_near(k).wait_send()

        def sent(o, _):
            fwd_far(o).wait_send()
            return 0

        lax.fori_loop(2, peers - 1, sent, 0)

    if with_back:
        for k in range(2):
            back_near(k).wait_send()

        def back_sent(d, _):
            back_far(d).wait_send()
            return 0

        lax.fori_loop(2, peers - 1, back_sent, 0)


def backward_kernel(src_ref, kern_ref, b_ref, part_ref, acc):
    r = pl.program_id(0)
    degree = kern_ref.shape[1]

    @pl.when(r == 0)
    def _():
        def clear(i, _):
            acc[i] = jnp.zeros(acc.shape[1:], F32)
            return 0

        lax.fori_loop(0, acc.shape[0], clear, 0)

    b = b_ref[r]
    for k in range(degree):
        prod = lax.dot_general(
            kern_ref[0, k], b, (((0,), (0,)), ((), ())), preferred_element_type=F32
        )
        acc[src_ref[r * degree + k]] += prod

    @pl.when(r == pl.num_programs(0) - 1)
    def _():
        def store(i, _):
            part_ref[i] = acc[i].astype(BF16)
            return 0

        lax.fori_loop(0, acc.shape[0], store, 0)


def per_device(kern_blocks, kern_cols, state_kernel, start_v, mu, nu):
    rows, degree, size, _ = kern_blocks.shape
    local_rows, cols = start_v.shape
    peers = lax.axis_size("mesh")
    states = lax.axis_size("state")
    me = lax.axis_index("mesh")
    per = rows // states
    nfar = (peers - 3) * FAR
    table_size = rows + 2 * NEAR + nfar
    nodes = states * cols
    sources, requests = far_plan(kern_cols.reshape(-1), me, peers, rows)
    asked = lax.all_to_all(requests, "mesh", split_axis=0, concat_axis=0, tiled=True).reshape(-1)
    perm, keep, last = arrival_order(asked, me, peers, rows)
    nu_blocks = nu.reshape(rows, size, cols)
    dma = pltpu.SemaphoreType.DMA

    def blk(*dims, dtype=BF16):
        return jax.ShapeDtypeStruct(dims + (size, cols), dtype)

    def scratch(*dims, dtype=BF16):
        return pltpu.VMEM(dims + (size, cols), dtype)

    def exchange(mode, with_u, ident, parts):
        ins, specs, outs, scr = [], [], [], []
        if mode == "first":
            ins += [start_v.reshape(rows, size, cols)]
            specs += [vmem()]
        else:
            ins += [perm, keep, last, parts, nu_blocks]
            specs += [smem(), smem(), smem(), hbm(), hbm()]
            scr += [
                scratch(rows), scratch(2 * NEAR + nfar), scratch(nfar, dtype=F32),
                scratch(rows, dtype=F32), dma((peers,)), dma((peers,)), dma((2,)),
            ]
        if mode == "last":
            outs += [blk(rows, dtype=F32)]
        else:
            ins += [asked, sources, kern_blocks, state_kernel, mu]
            specs += [smem(), smem(), hbm(), hbm(), hbm()]
            outs += [blk(rows)]
            if with_u:
                outs += [jax.ShapeDtypeStruct((local_rows // states, nodes), F32)]
            scr += [
                scratch(table_size), scratch(rows), scratch(peers * FAR),
                pltpu.VMEM((rows, degree, size, size), BF16),
                pltpu.VMEM((nodes, nodes), BF16),
                pltpu.VMEM((local_rows // states, nodes), F32),
                scratch(states, per), scratch(states, per), scratch(states, per), scratch(states, per),
                dma, dma, dma, dma((2,)), dma((2,)), dma((peers,)), dma((peers,)),
                dma((states, per)), dma((states, per)), dma((states, per)), dma((states, per)),
            ]
        return pl.pallas_call(
            functools.partial(exchange_kernel, mode, with_u, peers, states),
            out_shape=tuple(outs),
            in_specs=specs,
            out_specs=tuple(vmem() for _ in outs),
            scratch_shapes=scr,
            compiler_params=pltpu.CompilerParams(
                vmem_limit_bytes=VMEM_LIMIT, collective_id=ident, has_side_effects=True
            ),
            name="exchange_" + mode,
        )(*ins)

    def backward(b):
        return pl.pallas_call(
            backward_kernel,
            grid_spec=pltpu.PrefetchScalarGridSpec(
                num_scalar_prefetch=1,
                grid=(rows,),
                in_specs=[
                    pl.BlockSpec((1, degree, size, size), lambda r, s: (r, 0, 0, 0)),
                    pl.BlockSpec((rows, size, cols), lambda r, s: (0, 0, 0)),
                ],
                out_specs=pl.BlockSpec((table_size, size, cols), lambda r, s: (0, 0, 0)),
                scratch_shapes=[scratch(table_size, dtype=F32)],
            ),
            out_shape=blk(table_size),
            compiler_params=pltpu.CompilerParams(vmem_limit_bytes=VMEM_LIMIT),
            name="backward",
        )(sources, kern_blocks, b)

    result = exchange("first", ITERS == 1, 0, None)
    for sweep in range(1, ITERS):
        result = exchange("mid", sweep == ITERS - 1, sweep, backward(result[0]))
    potential_u = result[1]
    (values,) = exchange("last", False, ITERS, backward(result[0]))
    return (potential_u, values.reshape(local_rows, cols))


def solution(mesh):
    placed = (
        P("mesh", None, None, None),
        P("mesh", None),
        P(),
        P("mesh", "state"),
        P(("mesh", "state"), None),
        P("mesh", "state"),
    )
    return jax.shard_map(
        per_device,
        mesh=mesh,
        in_specs=placed,
        out_specs=(P(("mesh", "state"), None), P("mesh", "state")),
        check_vma=False,
    )
```

```python
import functools
import jax
import jax.numpy as jnp
from jax import lax
from jax.experimental import pallas as pl
from jax.experimental.pallas import tpu as pltpu
from jax.sharding import PartitionSpec as P

ITERS = 2
NEAR = 6
FAR = 2
LAG = 2
VMEM_LIMIT = 60 * 1024 * 1024
F32 = jnp.float32
BF16 = jnp.bfloat16


def vmem():
    return pl.BlockSpec(memory_space=pltpu.VMEM)


def smem():
    return pl.BlockSpec(memory_space=pltpu.SMEM)


def hbm():
    return pl.BlockSpec(memory_space=pl.ANY)


def far_plan(flat_cols, me, peers, rows):
    owners = flat_cols // rows
    places = flat_cols % rows
    delta = (owners - me + peers) % peers
    is_own = delta == 0
    is_left = delta == peers - 1
    is_right = delta == 1
    is_far = ~(is_own | is_left | is_right)
    ids = jnp.arange(peers * rows, dtype=jnp.int32)
    hits = (flat_cols[:, None] == ids[None, :]) & is_far[:, None]
    needed = jnp.max(hits.astype(jnp.int32), axis=0).reshape(peers, rows)
    before = jnp.arange(rows)[:, None] < jnp.arange(rows)[None, :]
    ranks = jnp.sum(needed[:, :, None] * before[None].astype(jnp.int32), axis=1)
    place_ids = jnp.arange(rows, dtype=jnp.int32)
    requests = jnp.stack(
        [jnp.sum(needed * (ranks == s) * place_ids[None, :], axis=1) for s in range(FAR)],
        axis=1,
    )
    slots = jnp.sum(hits.astype(jnp.int32) * ranks.reshape(1, -1), axis=1)
    far_at = rows + 2 * NEAR + (delta - 2) * FAR + slots
    sources = jnp.where(
        is_own,
        places,
        jnp.where(
            is_left,
            rows + places - (rows - NEAR),
            jnp.where(is_right, rows + NEAR + places, far_at),
        ),
    )
    return sources.astype(jnp.int32), requests.astype(jnp.int32)


def ordered_sums(keys, bins):
    count = keys.shape[0]
    ids = jnp.arange(count, dtype=jnp.int32)
    full = keys * count + ids
    rank = jnp.sum((full[None, :] < full[:, None]).astype(jnp.int32), axis=1)
    here = (rank[:, None] == ids[None, :]).astype(jnp.int32)
    perm = jnp.sum(here * ids[:, None], axis=0)
    bin_ids = jnp.arange(bins, dtype=jnp.int32)[:, None]
    upto = jnp.sum((keys[None, :] <= bin_ids).astype(jnp.int32), axis=1)
    some = jnp.any(keys[None, :] == bin_ids, axis=1)
    return perm, jnp.where(some, upto - 1, -1)


def ask_kernel(peers, want_ref, got_ref, inbox, send_sem, recv_sem):
    me = lax.axis_index("mesh")
    barrier = pltpu.get_barrier_semaphore()

    def greet(o, _):
        pl.semaphore_signal(barrier, inc=1, device_id={"mesh": lax.rem(me + o, peers)})
        return 0

    lax.fori_loop(1, peers, greet, 0)
    pl.semaphore_wait(barrier, peers - 1)

    def ask(o):
        q = lax.rem(me + o, peers)
        return pltpu.make_async_remote_copy(
            src_ref=want_ref.at[q],
            dst_ref=inbox.at[me],
            send_sem=send_sem.at[o],
            recv_sem=recv_sem.at[o],
            device_id={"mesh": q},
        )

    def start(o, _):
        ask(o).start()
        return 0

    def wait(o, _):
        ask(o).wait_recv()
        ask(o).wait_send()
        return 0

    inbox[me] = want_ref[me]
    lax.fori_loop(1, peers, start, 0)
    lax.fori_loop(1, peers, wait, 0)
    got_ref[...] = inbox[...]


def solve_kernel(
    sweeps, peers, states,
    asked_ref, arr_perm, arr_last, arr_place, src_ref, pair_perm, pair_last,
    start_hbm, kern_hbm, mix_hbm, mu_hbm, nu_hbm,
    u_hbm, v_hbm,
    kern, mix, u_ref, v_ref, table, blocks, outbox, products, sums, arrived, running,
    a_out, a_in, b_out, b_in,
    local_sem, near_send, near_recv, far_send, far_recv,
    back_near_send, back_near_recv, back_far_send, back_far_recv,
    a_send, a_recv, b_send, b_recv,
):
    me = lax.axis_index("mesh")
    mz = lax.axis_index("state")
    rows, degree, size, _ = kern.shape
    cols = table.shape[2]
    per = rows // states
    far0 = rows + 2 * NEAR
    others = peers - 3
    right = lax.rem(me + 1, peers)
    left = lax.rem(me + peers - 1, peers)

    kern_copy = pltpu.make_async_copy(kern_hbm, kern, local_sem.at[0])
    mix_copy = pltpu.make_async_copy(mix_hbm, mix, local_sem.at[1])
    mu_copy = pltpu.make_async_copy(mu_hbm, u_ref, local_sem.at[2])
    nu_copy = pltpu.make_async_copy(nu_hbm, v_ref, local_sem.at[3])
    u_copy = pltpu.make_async_copy(u_ref, u_hbm, local_sem.at[4])
    v_copy = pltpu.make_async_copy(v_ref, v_hbm, local_sem.at[5])
    start_copy = pltpu.make_async_copy(start_hbm, v_ref, local_sem.at[6])
    start_copy.start()

    barrier = pltpu.get_barrier_semaphore()

    def greet(o, _):
        pl.semaphore_signal(barrier, inc=1, device_id={"mesh": lax.rem(me + o, peers)})
        return 0

    lax.fori_loop(1, peers, greet, 0)
    for j in range(1, states):
        pl.semaphore_signal(barrier, inc=1, device_id={"state": lax.rem(mz + j, states)})

    start_copy.wait()
    kern_copy.start()
    mix_copy.start()

    def cast(p, _):
        v = v_ref[p].astype(BF16)
        table[p] = v
        blocks[p] = v
        return 0

    lax.fori_loop(0, rows, cast, 0)
    pl.semaphore_wait(barrier, peers - 1 + states - 1)

    def every(body):
        def one(i, _):
            body(2 + lax.rem(i * 12, others))
            return 0

        lax.fori_loop(0, others, one, 0)

    def fwd_near(k):
        return pltpu.make_async_remote_copy(
            src_ref=blocks.at[pl.ds((rows - NEAR, 0)[k], NEAR)],
            dst_ref=table.at[pl.ds(rows + k * NEAR, NEAR)],
            send_sem=near_send.at[k],
            recv_sem=near_recv.at[k],
            device_id={"mesh": (right, left)[k]},
        )

    def fwd_far(o):
        at = peers - o
        return pltpu.make_async_remote_copy(
            src_ref=outbox.at[pl.ds(2 * NEAR + (o - 2) * FAR, FAR)],
            dst_ref=table.at[pl.ds(far0 + (at - 2) * FAR, FAR)],
            send_sem=far_send.at[o],
            recv_sem=far_recv.at[at],
            device_id={"mesh": lax.rem(me + o, peers)},
        )

    def back_near(k):
        return pltpu.make_async_remote_copy(
            src_ref=outbox.at[pl.ds(k * NEAR, NEAR)],
            dst_ref=arrived.at[pl.ds(k * NEAR, NEAR)],
            send_sem=back_near_send.at[k],
            recv_sem=back_near_recv.at[k],
            device_id={"mesh": (left, right)[k]},
        )

    def back_far(o):
        at = peers - o
        return pltpu.make_async_remote_copy(
            src_ref=outbox.at[pl.ds(2 * NEAR + (o - 2) * FAR, FAR)],
            dst_ref=arrived.at[pl.ds(2 * NEAR + (at - 2) * FAR, FAR)],
            send_sem=back_far_send.at[o],
            recv_sem=back_far_recv.at[at],
            device_id={"mesh": lax.rem(me + o, peers)},
        )

    def a_copy(j, sub):
        to = lax.rem(mz + j, states)
        return pltpu.make_async_remote_copy(
            src_ref=a_out.at[to, sub],
            dst_ref=a_in.at[mz, sub],
            send_sem=a_send.at[j, sub],
            recv_sem=a_recv.at[j, sub],
            device_id={"state": to},
        )

    def b_copy(j, sub):
        to = lax.rem(mz + j, states)
        return pltpu.make_async_remote_copy(
            src_ref=b_out.at[to, sub],
            dst_ref=b_in.at[mz, sub],
            send_sem=b_send.at[j, sub],
            recv_sem=b_recv.at[j, sub],
            device_id={"state": to},
        )

    def apply_rows(sub):
        for j in list(range(1, states)) + [0]:
            to = lax.rem(mz + j, states)
            r = to * per + sub
            lhs = jnp.concatenate([kern[r, k] for k in range(degree)], axis=1)
            rhs = jnp.concatenate(
                [table[src_ref[r * degree + k]] for k in range(degree)], axis=0
            )
            out = jnp.dot(lhs, rhs, preferred_element_type=F32).astype(BF16)
            if j == 0:
                a_in[mz, sub] = out
            else:
                a_out[to, sub] = out
                a_copy(j, sub).start()

    def mix_rows(sub):
        for j in range(1, states):
            a_copy(j, sub).wait_recv()
        a = jnp.concatenate([a_in[z, sub] for z in range(states)], axis=1)
        kv = lax.dot_general(a, mix[...], (((1,), (1,)), ((), ())), preferred_element_type=F32)
        at = pl.ds(pl.multiple_of(sub * size, size), size)
        u = u_ref[at, :] / kv
        u_ref[at, :] = u
        b = jnp.dot(u.astype(BF16), mix[...], preferred_element_type=F32).astype(BF16)
        for z in range(states):
            b_out[z, sub] = b[:, z * cols : (z + 1) * cols]
        for j in range(1, states):
            b_copy(j, sub).start()
        b_in[mz, sub] = b_out[mz, sub]

    def product_rows(sub):
        for j in range(1, states):
            b_copy(j, sub).wait_recv()
        for z in range(states):
            r = z * per + sub
            b = b_in[z, sub]
            for k in range(degree):
                products[r * degree + k] = lax.dot_general(
                    kern[r, k], b, (((0,), (0,)), ((), ())), preferred_element_type=F32
                ).astype(BF16)

    def chain(t, _):
        @pl.when(t < per)
        def _():
            apply_rows(t)

        @pl.when((t >= LAG) & (t < per + LAG))
        def _():
            mix_rows(t - LAG)

        @pl.when(t >= 2 * LAG)
        def _():
            product_rows(t - 2 * LAG)

        return 0

    def pick(ref, at):
        got = ref[jnp.maximum(at, 0)].astype(F32)
        return jnp.where(at >= 0, got, jnp.zeros_like(got))

    def sweep(s, _):
        mu_copy.start()
        nu_copy.start()

        def send(o):
            q = lax.rem(me + o, peers)
            for f in range(FAR):
                outbox[2 * NEAR + (o - 2) * FAR + f] = blocks[asked_ref[q * FAR + f]]
            fwd_far(o).start()

        for k in range(2):
            fwd_near(k).start()
        every(send)

        @pl.when(s == 0)
        def _():
            kern_copy.wait()
            mix_copy.wait()

        mu_copy.wait()
        nu_copy.wait()
        for k in range(2):
            fwd_near(k).wait_recv()
        every(lambda o: fwd_far(o).wait_recv())
        for k in range(2):
            fwd_near(k).wait_send()
        every(lambda o: fwd_far(o).wait_send())

        lax.fori_loop(0, per + 2 * LAG, chain, 0)
        u_copy.start()

        def add_pair(i, carry):
            acc, before = carry
            for h in range(4):
                p = pair_perm[i * 4 + h]
                now = src_ref[p]
                kept = jnp.where(now == before, acc, jnp.zeros_like(acc))
                acc = kept + products[p].astype(F32)
                sums[i * 4 + h] = acc.astype(BF16)
                before = now
            return acc, before

        lax.fori_loop(
            0, rows * degree // 4, add_pair, (jnp.zeros((size, cols), F32), jnp.int32(-1))
        )

        def pack_near(i, _):
            outbox[i] = pick(sums, pair_last[rows + i]).astype(BF16)
            return 0

        lax.fori_loop(0, 2 * NEAR, pack_near, 0)
        for k in range(2):
            back_near(k).start()

        def give(o):
            for f in range(FAR):
                i = 2 * NEAR + (o - 2) * FAR + f
                outbox[i] = pick(sums, pair_last[rows + i]).astype(BF16)
            back_far(o).start()

        every(give)

        def settle(sub, _):
            for j in range(1, states):
                a_copy(j, sub).wait_send()
                b_copy(j, sub).wait_send()
            return 0

        lax.fori_loop(0, per, settle, 0)
        u_copy.wait()
        for k in range(2):
            back_near(k).wait_recv()
        every(lambda o: back_far(o).wait_recv())
        for k in range(2):
            back_near(k).wait_send()
        every(lambda o: back_far(o).wait_send())

        def add_arrived(i, carry):
            acc, before = carry
            e = arr_perm[i]
            now = arr_place[e]
            kept = jnp.where(now == before, acc, jnp.zeros_like(acc))
            acc = kept + arrived[2 * NEAR + e].astype(F32)
            running[i] = acc
            return acc, now

        lax.fori_loop(
            0, others * FAR, add_arrived, (jnp.zeros((size, cols), F32), jnp.int32(-1))
        )

        def finish(p, near):
            total = pick(sums, pair_last[p]) + pick(running, arr_last[p])
            if near is not None:
                total = total + arrived[near].astype(F32)
            v = v_ref[p] / total
            v_ref[p] = v
            rounded = v.astype(BF16)
            table[p] = rounded
            blocks[p] = rounded
            return 0

        lax.fori_loop(0, NEAR, lambda p, _: finish(p, NEAR + p), 0)
        lax.fori_loop(NEAR, rows - NEAR, lambda p, _: finish(p, None), 0)
        lax.fori_loop(rows - NEAR, rows, lambda p, _: finish(p, p - (rows - NEAR)), 0)
        return 0

    lax.fori_loop(0, sweeps, sweep, 0)
    v_copy.start()
    v_copy.wait()


def per_device(kern_blocks, kern_cols, state_kernel, start_v, mu, nu):
    rows, degree, size, _ = kern_blocks.shape
    local_rows, cols = start_v.shape
    peers = lax.axis_size("mesh")
    states = lax.axis_size("state")
    me = lax.axis_index("mesh")
    per = rows // states
    nfar = (peers - 3) * FAR
    table_size = rows + 2 * NEAR + nfar
    nodes = states * cols
    dma = pltpu.SemaphoreType.DMA
    sources, requests = far_plan(kern_cols.reshape(-1), me, peers, rows)
    want = jnp.pad(requests, ((0, 0), (0, cols - FAR))).reshape(peers, 1, cols)
    got = pl.pallas_call(
        functools.partial(ask_kernel, peers),
        out_shape=jax.ShapeDtypeStruct((peers, 1, cols), jnp.int32),
        in_specs=[vmem()],
        out_specs=vmem(),
        scratch_shapes=[pltpu.VMEM((peers, 1, cols), jnp.int32), dma((peers,)), dma((peers,))],
        compiler_params=pltpu.CompilerParams(collective_id=0, has_side_effects=True),
        name="ask",
    )(want)
    asked = got[:, 0, :FAR]
    pair_perm, pair_last = ordered_sums(sources, table_size)
    deltas = (me + jnp.arange(2, peers - 1, dtype=jnp.int32)) % peers
    arr_place = asked[deltas].reshape(-1)
    arr_perm, arr_last = ordered_sums(arr_place, rows)

    def scratch(*dims, dtype=BF16):
        return pltpu.VMEM(dims + (size, cols), dtype)

    potential_u, values = pl.pallas_call(
        functools.partial(solve_kernel, ITERS, peers, states),
        out_shape=(
            jax.ShapeDtypeStruct((local_rows // states, nodes), F32),
            jax.ShapeDtypeStruct((rows, size, cols), F32),
        ),
        in_specs=[smem()] * 7 + [hbm()] * 5,
        out_specs=(hbm(), hbm()),
        scratch_shapes=[
            pltpu.VMEM((rows, degree, size, size), BF16),
            pltpu.VMEM((nodes, nodes), BF16),
            pltpu.VMEM((local_rows // states, nodes), F32),
            scratch(rows, dtype=F32),
            scratch(table_size),
            scratch(rows),
            scratch(2 * NEAR + nfar),
            scratch(rows * degree),
            scratch(rows * degree),
            scratch(2 * NEAR + nfar),
            scratch(nfar, dtype=F32),
            scratch(states, per),
            scratch(states, per),
            scratch(states, per),
            scratch(states, per),
            dma((7,)),
            dma((2,)), dma((2,)), dma((peers,)), dma((peers,)),
            dma((2,)), dma((2,)), dma((peers,)), dma((peers,)),
            dma((states, per)), dma((states, per)), dma((states, per)), dma((states, per)),
        ],
        compiler_params=pltpu.CompilerParams(
            vmem_limit_bytes=VMEM_LIMIT, collective_id=1, has_side_effects=True
        ),
        name="solve",
    )(
        asked.reshape(-1), arr_perm, arr_last, arr_place, sources, pair_perm, pair_last,
        start_v.reshape(rows, size, cols), kern_blocks, state_kernel, mu,
        nu.reshape(rows, size, cols),
    )
    return (potential_u, values.reshape(local_rows, cols))


def solution(mesh):
    placed = (
        P("mesh", None, None, None),
        P("mesh", None),
        P(),
        P("mesh", "state"),
        P(("mesh", "state"), None),
        P("mesh", "state"),
    )
    return jax.shard_map(
        per_device,
        mesh=mesh,
        in_specs=placed,
        out_specs=(P(("mesh", "state"), None), P("mesh", "state")),
        check_vma=False,
    )
```

```python
import functools
import jax
import jax.numpy as jnp
from jax import lax
from jax.experimental import pallas as pl
from jax.experimental.pallas import tpu as pltpu
from jax.sharding import PartitionSpec as P

ITERS = 2
NEAR = 6
FAR = 2
LAG = 2
VMEM_LIMIT = 60 * 1024 * 1024
F32 = jnp.float32
BF16 = jnp.bfloat16


def vmem():
    return pl.BlockSpec(memory_space=pltpu.VMEM)


def smem():
    return pl.BlockSpec(memory_space=pltpu.SMEM)


def hbm():
    return pl.BlockSpec(memory_space=pl.ANY)


def far_plan(flat_cols, me, peers, rows):
    owners = flat_cols // rows
    places = flat_cols % rows
    delta = (owners - me + peers) % peers
    is_own = delta == 0
    is_left = delta == peers - 1
    is_right = delta == 1
    is_far = ~(is_own | is_left | is_right)
    ids = jnp.arange(peers * rows, dtype=jnp.int32)
    hits = (flat_cols[:, None] == ids[None, :]) & is_far[:, None]
    needed = jnp.max(hits.astype(jnp.int32), axis=0).reshape(peers, rows)
    before = jnp.arange(rows)[:, None] < jnp.arange(rows)[None, :]
    ranks = jnp.sum(needed[:, :, None] * before[None].astype(jnp.int32), axis=1)
    place_ids = jnp.arange(rows, dtype=jnp.int32)
    requests = jnp.stack(
        [jnp.sum(needed * (ranks == s) * place_ids[None, :], axis=1) for s in range(FAR)],
        axis=1,
    )
    slots = jnp.sum(hits.astype(jnp.int32) * ranks.reshape(1, -1), axis=1)
    far_at = rows + 2 * NEAR + (delta - 2) * FAR + slots
    sources = jnp.where(
        is_own,
        places,
        jnp.where(
            is_left,
            rows + places - (rows - NEAR),
            jnp.where(is_right, rows + NEAR + places, far_at),
        ),
    )
    return sources.astype(jnp.int32), requests.astype(jnp.int32)


def ordered_sums(keys, bins):
    count = keys.shape[0]
    ids = jnp.arange(count, dtype=jnp.int32)
    full = keys * count + ids
    rank = jnp.sum((full[None, :] < full[:, None]).astype(jnp.int32), axis=1)
    here = (rank[:, None] == ids[None, :]).astype(jnp.int32)
    perm = jnp.sum(here * ids[:, None], axis=0)
    bin_ids = jnp.arange(bins, dtype=jnp.int32)[:, None]
    upto = jnp.sum((keys[None, :] <= bin_ids).astype(jnp.int32), axis=1)
    some = jnp.any(keys[None, :] == bin_ids, axis=1)
    return perm, jnp.where(some, upto - 1, -1)


def ask_kernel(peers, want_ref, got_ref, inbox, send_sem, recv_sem):
    me = lax.axis_index("mesh")
    barrier = pltpu.get_barrier_semaphore()

    def greet(o, _):
        pl.semaphore_signal(barrier, inc=1, device_id={"mesh": lax.rem(me + o, peers)})
        return 0

    lax.fori_loop(1, peers, greet, 0)
    pl.semaphore_wait(barrier, peers - 1)

    def ask(o):
        q = lax.rem(me + o, peers)
        return pltpu.make_async_remote_copy(
            src_ref=want_ref.at[q],
            dst_ref=inbox.at[me],
            send_sem=send_sem.at[o],
            recv_sem=recv_sem.at[o],
            device_id={"mesh": q},
        )

    def start(o, _):
        ask(o).start()
        return 0

    def wait(o, _):
        ask(o).wait_recv()
        ask(o).wait_send()
        return 0

    inbox[me] = want_ref[me]
    lax.fori_loop(1, peers, start, 0)
    lax.fori_loop(1, peers, wait, 0)
    got_ref[...] = inbox[...]


def solve_kernel(
    sweeps, peers, states,
    asked_ref, arr_perm, arr_last, arr_place, src_ref, pair_perm, pair_last,
    start_hbm, kern_hbm, mix_hbm, mix_t_hbm, mu_hbm, nu_hbm,
    u_ref, v_ref,
    kern, mix, mix_t, u_t, table_0, table_1, blocks_0, blocks_1, outbox, products, sums,
    arrived_0, arrived_1, running,
    a_out, a_in, b_out, b_in,
    local_sem, near_send, near_recv, far_send, far_recv,
    back_near_send, back_near_recv, back_far_send, back_far_recv,
    a_send, a_recv, b_send, b_recv,
):
    me = lax.axis_index("mesh")
    mz = lax.axis_index("state")
    rows, degree, size, _ = kern.shape
    table, blocks, arrived = (table_0, table_1), (blocks_0, blocks_1), (arrived_0, arrived_1)
    half = table_0.shape[1]
    per = rows // states
    far0 = rows + 2 * NEAR
    others = peers - 3
    right = lax.rem(me + 1, peers)
    left = lax.rem(me + peers - 1, peers)

    kern_copy = pltpu.make_async_copy(kern_hbm, kern, local_sem.at[0])
    mix_copy = pltpu.make_async_copy(mix_hbm, mix, local_sem.at[1])
    mix_t_copy = pltpu.make_async_copy(mix_t_hbm, mix_t, local_sem.at[2])
    mu_copy = pltpu.make_async_copy(mu_hbm, u_ref, local_sem.at[3])
    nu_copy = pltpu.make_async_copy(nu_hbm, v_ref, local_sem.at[4])
    start_copy = pltpu.make_async_copy(start_hbm, v_ref, local_sem.at[5])
    start_copy.start()

    barrier = pltpu.get_barrier_semaphore()

    def greet(o, _):
        pl.semaphore_signal(barrier, inc=1, device_id={"mesh": lax.rem(me + o, peers)})
        return 0

    lax.fori_loop(1, peers, greet, 0)
    for j in range(1, states):
        pl.semaphore_signal(barrier, inc=1, device_id={"state": lax.rem(mz + j, states)})

    start_copy.wait()
    kern_copy.start()
    mix_copy.start()
    mix_t_copy.start()

    def cast(p, _):
        v = v_ref[p].T.astype(BF16)
        for h in range(2):
            table[h][p] = v[h * half : (h + 1) * half]
            blocks[h][p] = v[h * half : (h + 1) * half]
        return 0

    lax.fori_loop(0, rows, cast, 0)
    pl.semaphore_wait(barrier, peers - 1 + states - 1)

    def every(body):
        def one(i, _):
            body(2 + lax.rem(i * 12, others))
            return 0

        lax.fori_loop(0, others, one, 0)

    def fwd_near(h, k):
        return pltpu.make_async_remote_copy(
            src_ref=blocks[h].at[pl.ds((rows - NEAR, 0)[k], NEAR)],
            dst_ref=table[h].at[pl.ds(rows + k * NEAR, NEAR)],
            send_sem=near_send.at[h, k],
            recv_sem=near_recv.at[h, k],
            device_id={"mesh": (right, left)[k]},
        )

    def fwd_far(h, o):
        at = peers - o
        return pltpu.make_async_remote_copy(
            src_ref=outbox.at[h, pl.ds(2 * NEAR + (o - 2) * FAR, FAR)],
            dst_ref=table[h].at[pl.ds(far0 + (at - 2) * FAR, FAR)],
            send_sem=far_send.at[h, o],
            recv_sem=far_recv.at[h, at],
            device_id={"mesh": lax.rem(me + o, peers)},
        )

    def back_near(h, k):
        return pltpu.make_async_remote_copy(
            src_ref=outbox.at[h, pl.ds(k * NEAR, NEAR)],
            dst_ref=arrived[h].at[pl.ds(k * NEAR, NEAR)],
            send_sem=back_near_send.at[h, k],
            recv_sem=back_near_recv.at[h, k],
            device_id={"mesh": (left, right)[k]},
        )

    def back_far(h, o):
        at = peers - o
        return pltpu.make_async_remote_copy(
            src_ref=outbox.at[h, pl.ds(2 * NEAR + (o - 2) * FAR, FAR)],
            dst_ref=arrived[h].at[pl.ds(2 * NEAR + (at - 2) * FAR, FAR)],
            send_sem=back_far_send.at[h, o],
            recv_sem=back_far_recv.at[h, at],
            device_id={"mesh": lax.rem(me + o, peers)},
        )

    def a_copy(h, j, sub):
        to = lax.rem(mz + j, states)
        return pltpu.make_async_remote_copy(
            src_ref=a_out.at[h, to, sub],
            dst_ref=a_in.at[h, mz, sub],
            send_sem=a_send.at[h, j, sub],
            recv_sem=a_recv.at[h, j, sub],
            device_id={"state": to},
        )

    def b_copy(h, j, sub):
        to = lax.rem(mz + j, states)
        return pltpu.make_async_remote_copy(
            src_ref=b_out.at[h, to, sub],
            dst_ref=b_in.at[h, mz, sub],
            send_sem=b_send.at[h, j, sub],
            recv_sem=b_recv.at[h, j, sub],
            device_id={"state": to},
        )

    def send_forward(h):
        for k in range(2):
            fwd_near(h, k).start()

        def send(o):
            q = lax.rem(me + o, peers)
            for f in range(FAR):
                outbox[h, 2 * NEAR + (o - 2) * FAR + f] = blocks[h][asked_ref[q * FAR + f]]
            fwd_far(h, o).start()

        every(send)

    def receive_forward(h):
        for k in range(2):
            fwd_near(h, k).wait_recv()
        every(lambda o: fwd_far(h, o).wait_recv())

    def forward_sent(h):
        for k in range(2):
            fwd_near(h, k).wait_send()
        every(lambda o: fwd_far(h, o).wait_send())

    def apply_rows(h, sub):
        for j in list(range(1, states)) + [0]:
            to = lax.rem(mz + j, states)
            r = to * per + sub
            lhs = jnp.concatenate(
                [table[h][src_ref[r * degree + k]] for k in range(degree)], axis=1
            )
            rhs = jnp.concatenate([kern[r, k] for k in range(degree)], axis=1)
            out = lax.dot_general(
                lhs, rhs, (((1,), (1,)), ((), ())), preferred_element_type=F32
            ).astype(BF16)
            if j == 0:
                a_in[h, mz, sub] = out
            else:
                a_out[h, to, sub] = out
                a_copy(h, j, sub).start()

    def mix_rows(sub):
        for h in range(2):
            for j in range(1, states):
                a_copy(h, j, sub).wait_recv()
        a = jnp.concatenate(
            [a_in[h, z, sub] for z in range(states) for h in range(2)], axis=0
        )
        kv = jnp.dot(mix[...], a, preferred_element_type=F32)
        at = pl.ds(pl.multiple_of(sub * size, size), size)
        u = u_ref[at, :].T / kv
        u_t[sub] = u
        b = jnp.dot(mix_t[...], u.astype(BF16), preferred_element_type=F32).astype(BF16)
        for z in range(states):
            for h in range(2):
                b_out[h, z, sub] = b[(2 * z + h) * half : (2 * z + h + 1) * half]
        for j in range(1, states):
            b_copy(0, j, sub).start()
        for h in range(2):
            b_in[h, mz, sub] = b_out[h, mz, sub]

    def product_rows(h, sub):
        for j in range(1, states):
            b_copy(h, j, sub).wait_recv()
        for z in range(states):
            r = z * per + sub
            b = b_in[h, z, sub]
            for k in range(0, degree, 2):
                rhs = jnp.concatenate([kern[r, k], kern[r, k + 1]], axis=1)
                both = jnp.dot(b, rhs, preferred_element_type=F32)
                products[r * degree + k] = both[:, :size]
                products[r * degree + k + 1] = both[:, size:]

    def chain(t, _):
        @pl.when(t < per)
        def _():
            apply_rows(1, t)

        @pl.when((t >= LAG) & (t < per + LAG))
        def _():
            mix_rows(t - LAG)

        @pl.when(t == per + LAG - 1)
        def _():
            def rest(sub, _):
                for j in range(1, states):
                    b_copy(1, j, sub).start()
                return 0

            lax.fori_loop(0, per, rest, 0)

        @pl.when(t >= 2 * LAG)
        def _():
            product_rows(0, t - 2 * LAG)

        return 0

    def zeros():
        return jnp.zeros((half, size), F32)

    def pick(got, at):
        return jnp.where(at >= 0, got.astype(F32), zeros())

    def sum_products(h):
        def add(i, carry):
            acc, before = carry
            for g in range(8):
                p = pair_perm[i * 8 + g]
                now = src_ref[p]
                acc = jnp.where(now == before, acc, zeros()) + products[p]
                sums[h, i * 8 + g] = acc.astype(BF16)
                before = now
            return acc, before

        lax.fori_loop(0, rows * degree // 8, add, (zeros(), jnp.int32(-1)))

    def send_back(h):
        def load(i):
            at = pair_last[rows + i]
            outbox[h, i] = pick(sums[h, jnp.maximum(at, 0)], at).astype(BF16)

        def pack_near(i, _):
            load(i)
            return 0

        lax.fori_loop(0, 2 * NEAR, pack_near, 0)
        for k in range(2):
            back_near(h, k).start()

        def give(o):
            for f in range(FAR):
                load(2 * NEAR + (o - 2) * FAR + f)
            back_far(h, o).start()

        every(give)

    def receive_back(h):
        for k in range(2):
            back_near(h, k).wait_recv()
        every(lambda o: back_far(h, o).wait_recv())
        for k in range(2):
            back_near(h, k).wait_send()
        every(lambda o: back_far(h, o).wait_send())

    def finish_all(h):
        def add(i, carry):
            acc, before = carry
            e = arr_perm[i]
            now = arr_place[e]
            acc = jnp.where(now == before, acc, zeros()) + arrived[h][2 * NEAR + e].astype(F32)
            running[i] = acc
            return acc, now

        lax.fori_loop(0, others * FAR, add, (zeros(), jnp.int32(-1)))

        def finish(p, near):
            at, far = pair_last[p], arr_last[p]
            total = pick(sums[h, jnp.maximum(at, 0)], at) + pick(running[jnp.maximum(far, 0)], far)
            if near is not None:
                total = total + arrived[h][near].astype(F32)
            v = v_ref[p, h * half : (h + 1) * half] / total
            v_ref[p, h * half : (h + 1) * half] = v
            rounded = v.astype(BF16)
            table[h][p] = rounded
            blocks[h][p] = rounded
            return 0

        lax.fori_loop(0, NEAR, lambda p, _: finish(p, NEAR + p), 0)
        lax.fori_loop(NEAR, rows - NEAR, lambda p, _: finish(p, None), 0)
        lax.fori_loop(rows - NEAR, rows, lambda p, _: finish(p, p - (rows - NEAR)), 0)

    for h in range(2):
        send_forward(h)

    def sweep(s, _):
        mu_copy.start()
        nu_copy.start()

        @pl.when(s == 0)
        def _():
            kern_copy.wait()
            mix_copy.wait()
            mix_t_copy.wait()

        mu_copy.wait()
        nu_copy.wait()

        def turn_nu(p, _):
            v_ref[p] = v_ref[p].T
            return 0

        lax.fori_loop(0, rows, turn_nu, 0)

        receive_forward(0)
        lax.fori_loop(0, per, lambda sub, _: (apply_rows(0, sub), 0)[1], 0)
        receive_forward(1)
        lax.fori_loop(0, per + 2 * LAG, chain, 0)
        for h in range(2):
            forward_sent(h)
        sum_products(0)
        send_back(0)
        lax.fori_loop(0, per, lambda sub, _: (product_rows(1, sub), 0)[1], 0)
        sum_products(1)
        send_back(1)

        def settle(sub, _):
            for h in range(2):
                for j in range(1, states):
                    a_copy(h, j, sub).wait_send()
                    b_copy(h, j, sub).wait_send()
            u_ref[pl.ds(pl.multiple_of(sub * size, size), size), :] = u_t[sub].T
            return 0

        lax.fori_loop(0, per, settle, 0)
        for h in range(2):
            receive_back(h)
            finish_all(h)

            @pl.when(s < sweeps - 1)
            def _():
                send_forward(h)

        return 0

    lax.fori_loop(0, sweeps, sweep, 0)


def per_device(kern_blocks, kern_cols, state_kernel, start_v, mu, nu):
    rows, degree, size, _ = kern_blocks.shape
    local_rows, cols = start_v.shape
    peers = lax.axis_size("mesh")
    states = lax.axis_size("state")
    me = lax.axis_index("mesh")
    per = rows // states
    nfar = (peers - 3) * FAR
    table_size = rows + 2 * NEAR + nfar
    nodes = states * cols
    dma = pltpu.SemaphoreType.DMA
    sources, requests = far_plan(kern_cols.reshape(-1), me, peers, rows)
    want = jnp.pad(requests, ((0, 0), (0, cols - FAR))).reshape(peers, 1, cols)
    got = pl.pallas_call(
        functools.partial(ask_kernel, peers),
        out_shape=jax.ShapeDtypeStruct((peers, 1, cols), jnp.int32),
        in_specs=[vmem()],
        out_specs=vmem(),
        scratch_shapes=[pltpu.VMEM((peers, 1, cols), jnp.int32), dma((peers,)), dma((peers,))],
        compiler_params=pltpu.CompilerParams(collective_id=0, has_side_effects=True),
        name="ask",
    )(want)
    asked = got[:, 0, :FAR]
    pair_perm, pair_last = ordered_sums(sources, table_size)
    deltas = (me + jnp.arange(2, peers - 1, dtype=jnp.int32)) % peers
    arr_place = asked[deltas].reshape(-1)
    arr_perm, arr_last = ordered_sums(arr_place, rows)

    half = cols // 2

    def scratch(*dims, dtype=BF16):
        return pltpu.VMEM(dims + (half, size), dtype)

    potential_u, values = pl.pallas_call(
        functools.partial(solve_kernel, ITERS, peers, states),
        out_shape=(
            jax.ShapeDtypeStruct((local_rows // states, nodes), F32),
            jax.ShapeDtypeStruct((rows, cols, size), F32),
        ),
        in_specs=[smem()] * 7 + [hbm()] * 6,
        out_specs=(vmem(), vmem()),
        scratch_shapes=[
            pltpu.VMEM((rows, degree, size, size), BF16),
            pltpu.VMEM((nodes, nodes), BF16),
            pltpu.VMEM((nodes, nodes), BF16),
            pltpu.VMEM((per, nodes, size), F32),
            scratch(table_size),
            scratch(table_size),
            scratch(rows),
            scratch(rows),
            scratch(2, 2 * NEAR + nfar),
            scratch(rows * degree, dtype=F32),
            scratch(2, rows * degree),
            scratch(2 * NEAR + nfar),
            scratch(2 * NEAR + nfar),
            scratch(nfar, dtype=F32),
            scratch(2, states, per),
            scratch(2, states, per),
            scratch(2, states, per),
            scratch(2, states, per),
            dma((6,)),
            dma((2, 2)), dma((2, 2)), dma((2, peers)), dma((2, peers)),
            dma((2, 2)), dma((2, 2)), dma((2, peers)), dma((2, peers)),
            dma((2, states, per)), dma((2, states, per)),
            dma((2, states, per)), dma((2, states, per)),
        ],
        compiler_params=pltpu.CompilerParams(
            vmem_limit_bytes=VMEM_LIMIT, collective_id=1, has_side_effects=True
        ),
        name="solve",
    )(
        asked.reshape(-1), arr_perm, arr_last, arr_place, sources, pair_perm, pair_last,
        start_v.reshape(rows, size, cols), kern_blocks, state_kernel, state_kernel.T, mu,
        nu.reshape(rows, size, cols),
    )
    return (potential_u, jnp.swapaxes(values, 1, 2).reshape(local_rows, cols))


def solution(mesh):
    placed = (
        P("mesh", None, None, None),
        P("mesh", None),
        P(),
        P("mesh", "state"),
        P(("mesh", "state"), None),
        P("mesh", "state"),
    )
    return jax.shard_map(
        per_device,
        mesh=mesh,
        in_specs=placed,
        out_specs=(P(("mesh", "state"), None), P("mesh", "state")),
        check_vma=False,
    )
```

```python
import functools
import jax
import jax.numpy as jnp
from jax import lax
from jax.experimental import pallas as pl
from jax.experimental.pallas import tpu as pltpu
from jax.sharding import PartitionSpec as P

ITERS = 2
NEAR = 6
FAR = 2
LAG = 2
VMEM_LIMIT = 60 * 1024 * 1024
F32 = jnp.float32
BF16 = jnp.bfloat16


def vmem():
    return pl.BlockSpec(memory_space=pltpu.VMEM)


def smem():
    return pl.BlockSpec(memory_space=pltpu.SMEM)


def hbm():
    return pl.BlockSpec(memory_space=pl.ANY)


def far_plan(flat_cols, me, peers, rows):
    owners = flat_cols // rows
    places = flat_cols % rows
    delta = (owners - me + peers) % peers
    is_own = delta == 0
    is_left = delta == peers - 1
    is_right = delta == 1
    is_far = ~(is_own | is_left | is_right)
    ids = jnp.arange(peers * rows, dtype=jnp.int32)
    hits = (flat_cols[:, None] == ids[None, :]) & is_far[:, None]
    needed = jnp.max(hits.astype(jnp.int32), axis=0).reshape(peers, rows)
    before = jnp.arange(rows)[:, None] < jnp.arange(rows)[None, :]
    ranks = jnp.sum(needed[:, :, None] * before[None].astype(jnp.int32), axis=1)
    place_ids = jnp.arange(rows, dtype=jnp.int32)
    requests = jnp.stack(
        [jnp.sum(needed * (ranks == s) * place_ids[None, :], axis=1) for s in range(FAR)],
        axis=1,
    )
    slots = jnp.sum(hits.astype(jnp.int32) * ranks.reshape(1, -1), axis=1)
    far_at = rows + 2 * NEAR + (delta - 2) * FAR + slots
    sources = jnp.where(
        is_own,
        places,
        jnp.where(
            is_left,
            rows + places - (rows - NEAR),
            jnp.where(is_right, rows + NEAR + places, far_at),
        ),
    )
    return sources.astype(jnp.int32), requests.astype(jnp.int32)


def ordered_sums(keys, bins):
    count = keys.shape[0]
    ids = jnp.arange(count, dtype=jnp.int32)
    full = keys * count + ids
    rank = jnp.sum((full[None, :] < full[:, None]).astype(jnp.int32), axis=1)
    here = (rank[:, None] == ids[None, :]).astype(jnp.int32)
    perm = jnp.sum(here * ids[:, None], axis=0)
    bin_ids = jnp.arange(bins, dtype=jnp.int32)[:, None]
    upto = jnp.sum((keys[None, :] <= bin_ids).astype(jnp.int32), axis=1)
    some = jnp.any(keys[None, :] == bin_ids, axis=1)
    return perm, jnp.where(some, upto - 1, -1)


def solve_kernel(
    sweeps, peers, states,
    want_ref, src_ref, pair_perm, pair_last,
    start_hbm, kern_hbm, mix_hbm, mix_t_hbm, mu_hbm, nu_hbm,
    u_ref, v_ref,
    kern, mix, mix_t, u_t, table_0, table_1, blocks_0, blocks_1, outbox, products, sums,
    arrived_0, arrived_1, running, inbox, asked, arr_key, arr_count,
    a_out, a_in, b_out, b_in,
    local_sem, near_send, near_recv, far_send, far_recv,
    back_near_send, back_near_recv, back_far_send, back_far_recv,
    a_send, a_recv, b_send, b_recv, ask_send, ask_recv,
):
    me = lax.axis_index("mesh")
    mz = lax.axis_index("state")
    rows, degree, size, _ = kern.shape
    table, blocks, arrived = (table_0, table_1), (blocks_0, blocks_1), (arrived_0, arrived_1)
    half = table_0.shape[1]
    per = rows // states
    far0 = rows + 2 * NEAR
    others = peers - 3
    right = lax.rem(me + 1, peers)
    left = lax.rem(me + peers - 1, peers)

    kern_copy = pltpu.make_async_copy(kern_hbm, kern, local_sem.at[0])
    mix_copy = pltpu.make_async_copy(mix_hbm, mix, local_sem.at[1])
    mix_t_copy = pltpu.make_async_copy(mix_t_hbm, mix_t, local_sem.at[2])
    mu_copy = pltpu.make_async_copy(mu_hbm, u_ref, local_sem.at[3])
    nu_copy = pltpu.make_async_copy(nu_hbm, v_ref, local_sem.at[4])
    start_copy = pltpu.make_async_copy(start_hbm, v_ref, local_sem.at[5])
    start_copy.start()

    barrier = pltpu.get_barrier_semaphore()

    def greet(o, _):
        pl.semaphore_signal(barrier, inc=1, device_id={"mesh": lax.rem(me + o, peers)})
        return 0

    lax.fori_loop(1, peers, greet, 0)
    for j in range(1, states):
        pl.semaphore_signal(barrier, inc=1, device_id={"state": lax.rem(mz + j, states)})

    def ask(o):
        q = lax.rem(me + o, peers)
        return pltpu.make_async_remote_copy(
            src_ref=want_ref.at[q],
            dst_ref=inbox.at[me],
            send_sem=ask_send.at[o],
            recv_sem=ask_recv.at[o],
            device_id={"mesh": q},
        )

    def ask_start(o, _):
        ask(o).start()
        return 0

    def ask_wait(o, _):
        ask(o).wait_recv()
        ask(o).wait_send()
        return 0

    inbox[me] = want_ref[me]
    pl.semaphore_wait(barrier, peers - 1 + states - 1)
    lax.fori_loop(1, peers, ask_start, 0)
    start_copy.wait()
    kern_copy.start()
    mix_copy.start()
    mix_t_copy.start()

    def cast(p, _):
        v = v_ref[p].T.astype(BF16)
        for h in range(2):
            table[h][p] = v[h * half : (h + 1) * half]
            blocks[h][p] = v[h * half : (h + 1) * half]
        return 0

    lax.fori_loop(0, rows, cast, 0)
    lax.fori_loop(1, peers, ask_wait, 0)
    asked_copy = pltpu.make_async_copy(inbox, asked, local_sem.at[6])
    asked_copy.start()
    asked_copy.wait()

    def every(body):
        def one(i, _):
            body(2 + lax.rem(i * 12, others))
            return 0

        lax.fori_loop(0, others, one, 0)

    def fwd_near(h, k):
        return pltpu.make_async_remote_copy(
            src_ref=blocks[h].at[pl.ds((rows - NEAR, 0)[k], NEAR)],
            dst_ref=table[h].at[pl.ds(rows + k * NEAR, NEAR)],
            send_sem=near_send.at[h, k],
            recv_sem=near_recv.at[h, k],
            device_id={"mesh": (right, left)[k]},
        )

    def fwd_far(h, o):
        at = peers - o
        return pltpu.make_async_remote_copy(
            src_ref=outbox.at[h, pl.ds(2 * NEAR + (o - 2) * FAR, FAR)],
            dst_ref=table[h].at[pl.ds(far0 + (at - 2) * FAR, FAR)],
            send_sem=far_send.at[h, o],
            recv_sem=far_recv.at[h, at],
            device_id={"mesh": lax.rem(me + o, peers)},
        )

    def back_near(h, k):
        return pltpu.make_async_remote_copy(
            src_ref=outbox.at[h, pl.ds(k * NEAR, NEAR)],
            dst_ref=arrived[h].at[pl.ds(k * NEAR, NEAR)],
            send_sem=back_near_send.at[h, k],
            recv_sem=back_near_recv.at[h, k],
            device_id={"mesh": (left, right)[k]},
        )

    def back_far(h, o):
        at = peers - o
        return pltpu.make_async_remote_copy(
            src_ref=outbox.at[h, pl.ds(2 * NEAR + (o - 2) * FAR, FAR)],
            dst_ref=arrived[h].at[pl.ds(2 * NEAR + (at - 2) * FAR, FAR)],
            send_sem=back_far_send.at[h, o],
            recv_sem=back_far_recv.at[h, at],
            device_id={"mesh": lax.rem(me + o, peers)},
        )

    def a_copy(h, j, sub):
        to = lax.rem(mz + j, states)
        return pltpu.make_async_remote_copy(
            src_ref=a_out.at[h, to, sub],
            dst_ref=a_in.at[h, mz, sub],
            send_sem=a_send.at[h, j, sub],
            recv_sem=a_recv.at[h, j, sub],
            device_id={"state": to},
        )

    def b_copy(h, j, sub):
        to = lax.rem(mz + j, states)
        return pltpu.make_async_remote_copy(
            src_ref=b_out.at[h, to, sub],
            dst_ref=b_in.at[h, mz, sub],
            send_sem=b_send.at[h, j, sub],
            recv_sem=b_recv.at[h, j, sub],
            device_id={"state": to},
        )

    def send_forward(h):
        for k in range(2):
            fwd_near(h, k).start()

        def send(o):
            q = lax.rem(me + o, peers)
            for f in range(FAR):
                outbox[h, 2 * NEAR + (o - 2) * FAR + f] = blocks[h][asked[q, 0, f]]
            fwd_far(h, o).start()

        every(send)

    def receive_forward(h):
        for k in range(2):
            fwd_near(h, k).wait_recv()
        every(lambda o: fwd_far(h, o).wait_recv())

    def forward_sent(h):
        for k in range(2):
            fwd_near(h, k).wait_send()
        every(lambda o: fwd_far(h, o).wait_send())

    def apply_rows(h, sub):
        for j in list(range(1, states)) + [0]:
            to = lax.rem(mz + j, states)
            r = to * per + sub
            lhs = jnp.concatenate(
                [table[h][src_ref[r * degree + k]] for k in range(degree)], axis=1
            )
            rhs = jnp.concatenate([kern[r, k] for k in range(degree)], axis=1)
            out = lax.dot_general(
                lhs, rhs, (((1,), (1,)), ((), ())), preferred_element_type=F32
            ).astype(BF16)
            if j == 0:
                a_in[h, mz, sub] = out
            else:
                a_out[h, to, sub] = out
                a_copy(h, j, sub).start()

    def mix_rows(sub):
        for h in range(2):
            for j in range(1, states):
                a_copy(h, j, sub).wait_recv()
        a = jnp.concatenate(
            [a_in[h, z, sub] for z in range(states) for h in range(2)], axis=0
        )
        kv = jnp.dot(mix[...], a, preferred_element_type=F32)
        at = pl.ds(pl.multiple_of(sub * size, size), size)
        u = u_ref[at, :].T / kv
        u_t[sub] = u
        b = jnp.dot(mix_t[...], u.astype(BF16), preferred_element_type=F32).astype(BF16)
        for z in range(states):
            for h in range(2):
                b_out[h, z, sub] = b[(2 * z + h) * half : (2 * z + h + 1) * half]
        for j in range(1, states):
            b_copy(0, j, sub).start()
        for h in range(2):
            b_in[h, mz, sub] = b_out[h, mz, sub]

    def product_rows(h, sub):
        for j in range(1, states):
            b_copy(h, j, sub).wait_recv()
        for z in range(states):
            r = z * per + sub
            b = b_in[h, z, sub]
            for k in range(0, degree, 2):
                rhs = jnp.concatenate([kern[r, k], kern[r, k + 1]], axis=1)
                both = jnp.dot(b, rhs, preferred_element_type=F32)
                products[r * degree + k] = both[:, :size]
                products[r * degree + k + 1] = both[:, size:]

    def chain(t, _):
        @pl.when(t < per)
        def _():
            apply_rows(1, t)

        @pl.when((t >= LAG) & (t < per + LAG))
        def _():
            mix_rows(t - LAG)

        @pl.when(t == per + LAG - 1)
        def _():
            def rest(sub, _):
                for j in range(1, states):
                    b_copy(1, j, sub).start()
                return 0

            lax.fori_loop(0, per, rest, 0)

        @pl.when(t >= 2 * LAG)
        def _():
            product_rows(0, t - 2 * LAG)

        return 0

    def zeros():
        return jnp.zeros((half, size), F32)

    def pick(got, at):
        return jnp.where(at >= 0, got.astype(F32), zeros())

    def sum_products(h):
        def add(i, carry):
            acc, before = carry
            for g in range(8):
                p = pair_perm[i * 8 + g]
                now = src_ref[p]
                acc = jnp.where(now == before, acc, zeros()) + products[p]
                sums[h, i * 8 + g] = acc.astype(BF16)
                before = now
            return acc, before

        lax.fori_loop(0, rows * degree // 8, add, (zeros(), jnp.int32(-1)))

    def send_back(h):
        def load(i):
            at = pair_last[rows + i]
            outbox[h, i] = pick(sums[h, jnp.maximum(at, 0)], at).astype(BF16)

        def pack_near(i, _):
            load(i)
            return 0

        lax.fori_loop(0, 2 * NEAR, pack_near, 0)
        for k in range(2):
            back_near(h, k).start()

        def give(o):
            for f in range(FAR):
                load(2 * NEAR + (o - 2) * FAR + f)
            back_far(h, o).start()

        every(give)

    def receive_back(h):
        for k in range(2):
            back_near(h, k).wait_recv()
        every(lambda o: back_far(h, o).wait_recv())
        for k in range(2):
            back_near(h, k).wait_send()
        every(lambda o: back_far(h, o).wait_send())

    def finish_all(h):
        def add(i, carry):
            acc, before = carry
            e = lax.rem(arr_key[i], base)
            now = arr_key[i] // base
            acc = jnp.where(now == before, acc, zeros()) + arrived[h][2 * NEAR + e].astype(F32)
            running[i] = acc
            return acc, now

        lax.fori_loop(0, others * FAR, add, (zeros(), jnp.int32(-1)))

        def finish(p, near):
            at = pair_last[p]
            far = jnp.where(arr_count[p + 1] > arr_count[p], arr_count[p + 1] - 1, -1)
            total = pick(sums[h, jnp.maximum(at, 0)], at) + pick(running[jnp.maximum(far, 0)], far)
            if near is not None:
                total = total + arrived[h][near].astype(F32)
            v = v_ref[p, h * half : (h + 1) * half] / total
            v_ref[p, h * half : (h + 1) * half] = v
            rounded = v.astype(BF16)
            table[h][p] = rounded
            blocks[h][p] = rounded
            return 0

        lax.fori_loop(0, NEAR, lambda p, _: finish(p, NEAR + p), 0)
        lax.fori_loop(NEAR, rows - NEAR, lambda p, _: finish(p, None), 0)
        lax.fori_loop(rows - NEAR, rows, lambda p, _: finish(p, p - (rows - NEAR)), 0)

    for h in range(2):
        send_forward(h)

    base = peers * FAR
    peer_id = lax.broadcasted_iota(jnp.int32, inbox.shape, 0)
    lane = lax.broadcasted_iota(jnp.int32, inbox.shape, 2)
    ahead = lax.rem(peer_id - me + peers, peers)
    real = (lane < FAR) & (ahead >= 2) & (ahead <= peers - 2)
    beyond = rows * base
    keys = jnp.where(real, inbox[...] * base + (ahead - 2) * FAR + lane, beyond)

    def next_key(i, last):
        key = jnp.min(jnp.where(keys > last, keys, beyond))
        arr_key[i] = key
        return key

    lax.fori_loop(0, others * FAR, next_key, jnp.int32(-1))

    def count(p, _):
        arr_count[p] = jnp.sum((keys < p * base).astype(jnp.int32))
        return 0

    lax.fori_loop(0, rows + 1, count, 0)

    def sweep(s, _):
        mu_copy.start()
        nu_copy.start()

        @pl.when(s == 0)
        def _():
            kern_copy.wait()
            mix_copy.wait()
            mix_t_copy.wait()

        mu_copy.wait()
        nu_copy.wait()

        def turn_nu(p, _):
            v_ref[p] = v_ref[p].T
            return 0

        lax.fori_loop(0, rows, turn_nu, 0)

        receive_forward(0)
        lax.fori_loop(0, per, lambda sub, _: (apply_rows(0, sub), 0)[1], 0)
        receive_forward(1)
        lax.fori_loop(0, per + 2 * LAG, chain, 0)
        for h in range(2):
            forward_sent(h)
        sum_products(0)
        send_back(0)
        lax.fori_loop(0, per, lambda sub, _: (product_rows(1, sub), 0)[1], 0)
        sum_products(1)
        send_back(1)

        def settle(sub, _):
            for h in range(2):
                for j in range(1, states):
                    a_copy(h, j, sub).wait_send()
                    b_copy(h, j, sub).wait_send()
            u_ref[pl.ds(pl.multiple_of(sub * size, size), size), :] = u_t[sub].T
            return 0

        lax.fori_loop(0, per, settle, 0)
        for h in range(2):
            receive_back(h)
            finish_all(h)

            @pl.when(s < sweeps - 1)
            def _():
                send_forward(h)

        return 0

    lax.fori_loop(0, sweeps, sweep, 0)

    def turn_v(p, _):
        v_ref[p] = v_ref[p].T
        return 0

    lax.fori_loop(0, rows, turn_v, 0)


def per_device(kern_blocks, kern_cols, state_kernel, start_v, mu, nu):
    rows, degree, size, _ = kern_blocks.shape
    local_rows, cols = start_v.shape
    peers = lax.axis_size("mesh")
    states = lax.axis_size("state")
    me = lax.axis_index("mesh")
    per = rows // states
    nfar = (peers - 3) * FAR
    table_size = rows + 2 * NEAR + nfar
    nodes = states * cols
    dma = pltpu.SemaphoreType.DMA
    sources, requests = far_plan(kern_cols.reshape(-1), me, peers, rows)
    want = jnp.pad(requests, ((0, 0), (0, cols - FAR))).reshape(peers, 1, cols)
    pair_perm, pair_last = ordered_sums(sources, table_size)
    half = cols // 2

    def scratch(*dims, dtype=BF16):
        return pltpu.VMEM(dims + (half, size), dtype)

    potential_u, values = pl.pallas_call(
        functools.partial(solve_kernel, ITERS, peers, states),
        out_shape=(
            jax.ShapeDtypeStruct((local_rows // states, nodes), F32),
            jax.ShapeDtypeStruct((rows, size, cols), F32),
        ),
        in_specs=[vmem()] + [smem()] * 3 + [hbm()] * 6,
        out_specs=(vmem(), vmem()),
        scratch_shapes=[
            pltpu.VMEM((rows, degree, size, size), BF16),
            pltpu.VMEM((nodes, nodes), BF16),
            pltpu.VMEM((nodes, nodes), BF16),
            pltpu.VMEM((per, nodes, size), F32),
            scratch(table_size),
            scratch(table_size),
            scratch(rows),
            scratch(rows),
            scratch(2, 2 * NEAR + nfar),
            scratch(rows * degree, dtype=F32),
            scratch(2, rows * degree),
            scratch(2 * NEAR + nfar),
            scratch(2 * NEAR + nfar),
            scratch(nfar, dtype=F32),
            pltpu.VMEM((peers, 1, cols), jnp.int32),
            pltpu.SMEM((peers, 1, cols), jnp.int32),
            pltpu.SMEM((nfar,), jnp.int32),
            pltpu.SMEM((rows + 1,), jnp.int32),
            scratch(2, states, per),
            scratch(2, states, per),
            scratch(2, states, per),
            scratch(2, states, per),
            dma((7,)),
            dma((2, 2)), dma((2, 2)), dma((2, peers)), dma((2, peers)),
            dma((2, 2)), dma((2, 2)), dma((2, peers)), dma((2, peers)),
            dma((2, states, per)), dma((2, states, per)),
            dma((2, states, per)), dma((2, states, per)),
            dma((peers,)), dma((peers,)),
        ],
        compiler_params=pltpu.CompilerParams(
            vmem_limit_bytes=VMEM_LIMIT, collective_id=0, has_side_effects=True
        ),
        name="solve",
    )(
        want, sources, pair_perm, pair_last,
        start_v.reshape(rows, size, cols), kern_blocks, state_kernel, state_kernel.T, mu,
        nu.reshape(rows, size, cols),
    )
    return (potential_u, values.reshape(local_rows, cols))


def solution(mesh):
    placed = (
        P("mesh", None, None, None),
        P("mesh", None),
        P(),
        P("mesh", "state"),
        P(("mesh", "state"), None),
        P("mesh", "state"),
    )
    return jax.shard_map(
        per_device,
        mesh=mesh,
        in_specs=placed,
        out_specs=(P(("mesh", "state"), None), P("mesh", "state")),
        check_vma=False,
    )
```

```python
import functools
import jax
import jax.numpy as jnp
from jax import lax
from jax.experimental import pallas as pl
from jax.experimental.pallas import tpu as pltpu
from jax.sharding import PartitionSpec as P

ITERS = 2
NEAR = 6
FAR = 2
LAG = 1
VMEM_LIMIT = 60 * 1024 * 1024
F32 = jnp.float32
BF16 = jnp.bfloat16


def vmem():
    return pl.BlockSpec(memory_space=pltpu.VMEM)


def smem():
    return pl.BlockSpec(memory_space=pltpu.SMEM)


def hbm():
    return pl.BlockSpec(memory_space=pl.ANY)


def far_plan(flat_cols, me, peers, rows):
    owners = flat_cols // rows
    places = flat_cols % rows
    delta = (owners - me + peers) % peers
    is_own = delta == 0
    is_left = delta == peers - 1
    is_right = delta == 1
    is_far = ~(is_own | is_left | is_right)
    ids = jnp.arange(peers * rows, dtype=jnp.int32)
    hits = (flat_cols[:, None] == ids[None, :]) & is_far[:, None]
    needed = jnp.max(hits.astype(jnp.int32), axis=0).reshape(peers, rows)
    before = jnp.arange(rows)[:, None] < jnp.arange(rows)[None, :]
    ranks = jnp.sum(needed[:, :, None] * before[None].astype(jnp.int32), axis=1)
    place_ids = jnp.arange(rows, dtype=jnp.int32)
    requests = jnp.stack(
        [jnp.sum(needed * (ranks == s) * place_ids[None, :], axis=1) for s in range(FAR)],
        axis=1,
    )
    slots = jnp.sum(hits.astype(jnp.int32) * ranks.reshape(1, -1), axis=1)
    far_at = rows + 2 * NEAR + (delta - 2) * FAR + slots
    sources = jnp.where(
        is_own,
        places,
        jnp.where(
            is_left,
            rows + places - (rows - NEAR),
            jnp.where(is_right, rows + NEAR + places, far_at),
        ),
    )
    return sources.astype(jnp.int32), requests.astype(jnp.int32)


def ordered_sums(keys, bins):
    count = keys.shape[0]
    ids = jnp.arange(count, dtype=jnp.int32)
    full = keys * count + ids
    rank = jnp.sum((full[None, :] < full[:, None]).astype(jnp.int32), axis=1)
    here = (rank[:, None] == ids[None, :]).astype(jnp.int32)
    perm = jnp.sum(here * ids[:, None], axis=0)
    bin_ids = jnp.arange(bins, dtype=jnp.int32)[:, None]
    upto = jnp.sum((keys[None, :] <= bin_ids).astype(jnp.int32), axis=1)
    some = jnp.any(keys[None, :] == bin_ids, axis=1)
    return perm, jnp.where(some, upto - 1, -1)


def solve_kernel(
    sweeps, peers, states,
    want_ref, src_ref, pair_perm, pair_last,
    start_hbm, kern_hbm, mix_hbm, mu_hbm, nu_hbm,
    u_ref, v_ref,
    kern, mix, mix_t, mu_t, u_t, table_0, table_1, blocks_0, blocks_1, outbox, products, sums,
    arrived_0, arrived_1, running, inbox, packed, asked, arr_key, arr_count,
    a_out, a_in, b_out, b_in,
    local_sem, near_send, near_recv, far_send, far_recv,
    back_near_send, back_near_recv, back_far_send, back_far_recv,
    a_send, a_recv, b_send, b_recv, ask_send, ask_recv,
):
    me = lax.axis_index("mesh")
    mz = lax.axis_index("state")
    rows, degree, size, _ = kern.shape
    table, blocks, arrived = (table_0, table_1), (blocks_0, blocks_1), (arrived_0, arrived_1)
    half = table_0.shape[1]
    per = rows // states
    far0 = rows + 2 * NEAR
    others = peers - 3
    right = lax.rem(me + 1, peers)
    left = lax.rem(me + peers - 1, peers)

    kern_copy = pltpu.make_async_copy(kern_hbm, kern, local_sem.at[0])
    mix_copy = pltpu.make_async_copy(mix_hbm, mix, local_sem.at[1])
    mu_copy = pltpu.make_async_copy(mu_hbm, u_ref, local_sem.at[3])
    nu_copy = pltpu.make_async_copy(nu_hbm, v_ref, local_sem.at[4])
    start_copy = pltpu.make_async_copy(start_hbm, v_ref, local_sem.at[5])
    start_copy.start()

    barrier = pltpu.get_barrier_semaphore()

    def greet(o, _):
        pl.semaphore_signal(barrier, inc=1, device_id={"mesh": lax.rem(me + o, peers)})
        return 0

    lax.fori_loop(1, peers, greet, 0)
    for j in range(1, states):
        pl.semaphore_signal(barrier, inc=1, device_id={"state": lax.rem(mz + j, states)})

    def ask(o):
        q = lax.rem(me + o, peers)
        return pltpu.make_async_remote_copy(
            src_ref=want_ref.at[q],
            dst_ref=inbox.at[me],
            send_sem=ask_send.at[o],
            recv_sem=ask_recv.at[o],
            device_id={"mesh": q},
        )

    def ask_start(o, _):
        ask(o).start()
        return 0

    def ask_wait(o, _):
        ask(o).wait_recv()
        ask(o).wait_send()
        return 0

    inbox[me] = want_ref[me]
    pl.semaphore_wait(barrier, peers - 1 + states - 1)
    lax.fori_loop(1, peers, ask_start, 0)
    start_copy.wait()
    kern_copy.start()
    mix_copy.start()
    mu_copy.start()

    def cast(p, _):
        v = v_ref[p].astype(BF16).T
        for h in range(2):
            table[h][p] = v[h * half : (h + 1) * half]
            blocks[h][p] = v[h * half : (h + 1) * half]
        return 0

    lax.fori_loop(0, rows, cast, 0)
    lax.fori_loop(1, peers, ask_wait, 0)
    asked_copy = pltpu.make_async_copy(inbox, asked, local_sem.at[6])
    asked_copy.start()
    asked_copy.wait()

    def every(body):
        def one(i, _):
            body(2 + lax.rem(i * 12, others))
            return 0

        lax.fori_loop(0, others, one, 0)

    def fwd_near(h, k):
        return pltpu.make_async_remote_copy(
            src_ref=blocks[h].at[pl.ds((rows - NEAR, 0)[k], NEAR)],
            dst_ref=table[h].at[pl.ds(rows + k * NEAR, NEAR)],
            send_sem=near_send.at[h, k],
            recv_sem=near_recv.at[h, k],
            device_id={"mesh": (right, left)[k]},
        )

    def fwd_far(h, o):
        at = peers - o
        return pltpu.make_async_remote_copy(
            src_ref=outbox.at[h, pl.ds(2 * NEAR + (o - 2) * FAR, FAR)],
            dst_ref=table[h].at[pl.ds(far0 + (at - 2) * FAR, FAR)],
            send_sem=far_send.at[h, o],
            recv_sem=far_recv.at[h, at],
            device_id={"mesh": lax.rem(me + o, peers)},
        )

    def back_near(h, k):
        return pltpu.make_async_remote_copy(
            src_ref=outbox.at[h, pl.ds(k * NEAR, NEAR)],
            dst_ref=arrived[h].at[pl.ds(k * NEAR, NEAR)],
            send_sem=back_near_send.at[h, k],
            recv_sem=back_near_recv.at[h, k],
            device_id={"mesh": (left, right)[k]},
        )

    def back_far(h, o):
        at = peers - o
        return pltpu.make_async_remote_copy(
            src_ref=outbox.at[h, pl.ds(2 * NEAR + (o - 2) * FAR, FAR)],
            dst_ref=arrived[h].at[pl.ds(2 * NEAR + (at - 2) * FAR, FAR)],
            send_sem=back_far_send.at[h, o],
            recv_sem=back_far_recv.at[h, at],
            device_id={"mesh": lax.rem(me + o, peers)},
        )

    def a_copy(h, j, sub):
        to = lax.rem(mz + j, states)
        return pltpu.make_async_remote_copy(
            src_ref=a_out.at[h, to, sub],
            dst_ref=a_in.at[h, mz, sub],
            send_sem=a_send.at[h, j, sub],
            recv_sem=a_recv.at[h, j, sub],
            device_id={"state": to},
        )

    def b_copy(h, j, sub):
        to = lax.rem(mz + j, states)
        return pltpu.make_async_remote_copy(
            src_ref=b_out.at[h, to, sub],
            dst_ref=b_in.at[h, mz, sub],
            send_sem=b_send.at[h, j, sub],
            recv_sem=b_recv.at[h, j, sub],
            device_id={"state": to},
        )

    def send_forward(h):
        for k in range(2):
            fwd_near(h, k).start()

        def send(o):
            q = lax.rem(me + o, peers)
            for f in range(FAR):
                outbox[h, 2 * NEAR + (o - 2) * FAR + f] = blocks[h][asked[q, 0, f]]
            fwd_far(h, o).start()

        every(send)

    def receive_forward(h):
        for k in range(2):
            fwd_near(h, k).wait_recv()
        every(lambda o: fwd_far(h, o).wait_recv())

    def forward_sent(h):
        for k in range(2):
            fwd_near(h, k).wait_send()
        every(lambda o: fwd_far(h, o).wait_send())

    def apply_rows(h, sub):
        for j in list(range(1, states)) + [0]:
            to = lax.rem(mz + j, states)
            r = to * per + sub
            lhs = jnp.concatenate(
                [table[h][src_ref[r * degree + k]] for k in range(degree)], axis=1
            )
            rhs = jnp.concatenate([kern[r, k] for k in range(degree)], axis=1)
            out = lax.dot_general(
                lhs, rhs, (((1,), (1,)), ((), ())), preferred_element_type=F32
            ).astype(BF16)
            if j == 0:
                a_in[h, mz, sub] = out
            else:
                a_out[h, to, sub] = out
                a_copy(h, j, sub).start()

    def mix_rows(t):
        for i in range(2):
            for h in range(2):
                for j in range(1, states):
                    a_copy(h, j, 2 * t + i).wait_recv()
        a = jnp.concatenate(
            [
                jnp.concatenate([a_in[h, z, 2 * t + i] for i in range(2)], axis=1)
                for z in range(states)
                for h in range(2)
            ],
            axis=0,
        )
        kv = jnp.dot(mix[...], a, preferred_element_type=F32)
        u = mu_t[t] / kv
        u_t[t] = u
        b = jnp.dot(mix_t[...], u.astype(BF16), preferred_element_type=F32).astype(BF16)
        for i in range(2):
            for z in range(states):
                for h in range(2):
                    b_out[h, z, 2 * t + i] = b[
                        (2 * z + h) * half : (2 * z + h + 1) * half, i * size : (i + 1) * size
                    ]
            for j in range(1, states):
                b_copy(0, j, 2 * t + i).start()
            for h in range(2):
                b_in[h, mz, 2 * t + i] = b_out[h, mz, 2 * t + i]

    def product_rows(h, sub):
        for j in range(1, states):
            b_copy(h, j, sub).wait_recv()
        for z in range(states):
            r = z * per + sub
            b = b_in[h, z, sub]
            for k in range(0, degree, 2):
                rhs = jnp.concatenate([kern[r, k], kern[r, k + 1]], axis=1)
                both = jnp.dot(b, rhs, preferred_element_type=F32)
                products[r * degree + k] = both[:, :size]
                products[r * degree + k + 1] = both[:, size:]

    def chain(t, _):
        steps = per // 2

        @pl.when(t < steps)
        def _():
            for i in range(2):
                apply_rows(1, 2 * t + i)

        @pl.when((t >= LAG) & (t < steps + LAG))
        def _():
            mix_rows(t - LAG)

        @pl.when(t == steps + LAG - 1)
        def _():
            def rest(sub, _):
                for j in range(1, states):
                    b_copy(1, j, sub).start()
                return 0

            lax.fori_loop(0, per, rest, 0)

        @pl.when(t >= 2 * LAG)
        def _():
            for i in range(2):
                product_rows(0, 2 * (t - 2 * LAG) + i)

        return 0

    def zeros():
        return jnp.zeros((half, size), F32)

    def pick(got, at):
        return jnp.where(at >= 0, got.astype(F32), zeros())

    def sum_products(h):
        def add(i, carry):
            acc, before = carry
            for g in range(8):
                p = pair_perm[i * 8 + g]
                now = src_ref[p]
                acc = jnp.where(now == before, acc, zeros()) + products[p]
                sums[h, i * 8 + g] = acc.astype(BF16)
                before = now
            return acc, before

        lax.fori_loop(0, rows * degree // 8, add, (zeros(), jnp.int32(-1)))

    def send_back(h):
        def load(i):
            at = pair_last[rows + i]
            outbox[h, i] = pick(sums[h, jnp.maximum(at, 0)], at).astype(BF16)

        def pack_near(i, _):
            load(i)
            return 0

        lax.fori_loop(0, 2 * NEAR, pack_near, 0)
        for k in range(2):
            back_near(h, k).start()

        def give(o):
            for f in range(FAR):
                load(2 * NEAR + (o - 2) * FAR + f)
            back_far(h, o).start()

        every(give)

    def receive_back(h):
        for k in range(2):
            back_near(h, k).wait_recv()
        every(lambda o: back_far(h, o).wait_recv())
        for k in range(2):
            back_near(h, k).wait_send()
        every(lambda o: back_far(h, o).wait_send())

    def finish_all(h):
        def add(i, carry):
            acc, before = carry
            e = lax.rem(arr_key[i], base)
            now = arr_key[i] // base
            acc = jnp.where(now == before, acc, zeros()) + arrived[h][2 * NEAR + e].astype(F32)
            running[i] = acc
            return acc, now

        lax.fori_loop(0, others * FAR, add, (zeros(), jnp.int32(-1)))

        def finish(p, near):
            at = pair_last[p]
            far = jnp.where(arr_count[p + 1] > arr_count[p], arr_count[p + 1] - 1, -1)
            total = pick(sums[h, jnp.maximum(at, 0)], at) + pick(running[jnp.maximum(far, 0)], far)
            if near is not None:
                total = total + arrived[h][near].astype(F32)
            v = v_ref[p, h * half : (h + 1) * half] / total
            v_ref[p, h * half : (h + 1) * half] = v
            rounded = v.astype(BF16)
            table[h][p] = rounded
            blocks[h][p] = rounded
            return 0

        lax.fori_loop(0, NEAR, lambda p, _: finish(p, NEAR + p), 0)
        lax.fori_loop(NEAR, rows - NEAR, lambda p, _: finish(p, None), 0)
        lax.fori_loop(rows - NEAR, rows, lambda p, _: finish(p, p - (rows - NEAR)), 0)

    for h in range(2):
        send_forward(h)

    base = peers * FAR

    def order_arrivals():
        for q in range(peers):
            packed[q, :] = inbox[q, 0, :]
        peer_id = lax.broadcasted_iota(jnp.int32, packed.shape, 0)
        lane = lax.broadcasted_iota(jnp.int32, packed.shape, 1)
        ahead = lax.rem(peer_id - me + peers, peers)
        real = (lane < FAR) & (ahead >= 2) & (ahead <= peers - 2)
        beyond = rows * base
        keys = jnp.where(real, packed[...] * base + (ahead - 2) * FAR + lane, beyond)

        def next_key(i, last):
            key = jnp.min(jnp.where(keys > last, keys, beyond))
            arr_key[i] = key
            return key

        lax.fori_loop(0, others * FAR, next_key, jnp.int32(-1))
        arr_count[0] = 0

        def count(i, _):
            for g in range(4):
                p = i * 4 + g + 1
                arr_count[p] = jnp.sum((keys < p * base).astype(jnp.int32))
            return 0

        lax.fori_loop(0, rows // 4, count, 0)

    def sweep(s, _):
        nu_copy.start()

        @pl.when(s == 0)
        def _():
            mix_copy.wait()
            mu_copy.wait()
            for i in range(states):
                for j in range(states):
                    a, b = slice(i * size, (i + 1) * size), slice(j * size, (j + 1) * size)
                    mix_t[a, b] = mix[b, a].T

            def turn_mu(t, _):
                for i in range(2):
                    mu_t[t, :, i * size : (i + 1) * size] = u_ref[2 * t + i].T
                return 0

            lax.fori_loop(0, per // 2, turn_mu, 0)
            kern_copy.wait()

        nu_copy.wait()

        def turn_nu(p, _):
            v_ref[p] = v_ref[p].T
            return 0

        lax.fori_loop(0, rows, turn_nu, 0)

        receive_forward(0)
        lax.fori_loop(0, per, lambda sub, _: (apply_rows(0, sub), 0)[1], 0)

        @pl.when(s == 0)
        def _():
            order_arrivals()

        receive_forward(1)
        lax.fori_loop(0, per // 2 + 2 * LAG, chain, 0)
        for h in range(2):
            forward_sent(h)
        sum_products(0)
        send_back(0)
        lax.fori_loop(0, per, lambda sub, _: (product_rows(1, sub), 0)[1], 0)
        sum_products(1)
        send_back(1)

        def settle(sub, _):
            for h in range(2):
                for j in range(1, states):
                    a_copy(h, j, sub).wait_send()
                    b_copy(h, j, sub).wait_send()
            return 0

        lax.fori_loop(0, per, settle, 0)

        @pl.when(s == sweeps - 1)
        def _():
            def turn_u(t, _):
                for i in range(2):
                    u_ref[2 * t + i] = u_t[t, :, i * size : (i + 1) * size].T
                return 0

            lax.fori_loop(0, per // 2, turn_u, 0)

        for h in range(2):
            receive_back(h)
            finish_all(h)

            @pl.when(s < sweeps - 1)
            def _():
                send_forward(h)

        return 0

    lax.fori_loop(0, sweeps, sweep, 0)

    def turn_v(p, _):
        v_ref[p] = v_ref[p].T
        return 0

    lax.fori_loop(0, rows, turn_v, 0)


def per_device(kern_blocks, kern_cols, state_kernel, start_v, mu, nu):
    rows, degree, size, _ = kern_blocks.shape
    local_rows, cols = start_v.shape
    peers = lax.axis_size("mesh")
    states = lax.axis_size("state")
    me = lax.axis_index("mesh")
    per = rows // states
    nfar = (peers - 3) * FAR
    table_size = rows + 2 * NEAR + nfar
    nodes = states * cols
    dma = pltpu.SemaphoreType.DMA
    sources, requests = far_plan(kern_cols.reshape(-1), me, peers, rows)
    want = jnp.pad(requests, ((0, 0), (0, cols - FAR))).reshape(peers, 1, cols)
    pair_perm, pair_last = ordered_sums(sources, table_size)
    half = cols // 2

    def scratch(*dims, dtype=BF16):
        return pltpu.VMEM(dims + (half, size), dtype)

    potential_u, values = pl.pallas_call(
        functools.partial(solve_kernel, ITERS, peers, states),
        out_shape=(
            jax.ShapeDtypeStruct((per, size, nodes), F32),
            jax.ShapeDtypeStruct((rows, size, cols), F32),
        ),
        in_specs=[vmem()] + [smem()] * 3 + [hbm()] * 5,
        out_specs=(vmem(), vmem()),
        scratch_shapes=[
            pltpu.VMEM((rows, degree, size, size), BF16),
            pltpu.VMEM((nodes, nodes), BF16),
            pltpu.VMEM((nodes, nodes), BF16),
            pltpu.VMEM((per // 2, nodes, 2 * size), F32),
            pltpu.VMEM((per // 2, nodes, 2 * size), F32),
            scratch(table_size),
            scratch(table_size),
            scratch(rows),
            scratch(rows),
            scratch(2, 2 * NEAR + nfar),
            scratch(rows * degree, dtype=F32),
            scratch(2, rows * degree),
            scratch(2 * NEAR + nfar),
            scratch(2 * NEAR + nfar),
            scratch(nfar, dtype=F32),
            pltpu.VMEM((peers, 1, cols), jnp.int32),
            pltpu.VMEM((peers, cols), jnp.int32),
            pltpu.SMEM((peers, 1, cols), jnp.int32),
            pltpu.SMEM((nfar,), jnp.int32),
            pltpu.SMEM((rows + 1,), jnp.int32),
            scratch(2, states, per),
            scratch(2, states, per),
            scratch(2, states, per),
            scratch(2, states, per),
            dma((7,)),
            dma((2, 2)), dma((2, 2)), dma((2, peers)), dma((2, peers)),
            dma((2, 2)), dma((2, 2)), dma((2, peers)), dma((2, peers)),
            dma((2, states, per)), dma((2, states, per)),
            dma((2, states, per)), dma((2, states, per)),
            dma((peers,)), dma((peers,)),
        ],
        compiler_params=pltpu.CompilerParams(
            vmem_limit_bytes=VMEM_LIMIT, collective_id=0, has_side_effects=True
        ),
        name="solve",
    )(
        want, sources, pair_perm, pair_last,
        start_v.reshape(rows, size, cols), kern_blocks, state_kernel,
        mu.reshape(per, size, nodes),
        nu.reshape(rows, size, cols),
    )
    return (
        potential_u.reshape(local_rows // states, nodes),
        values.reshape(local_rows, cols),
    )


def solution(mesh):
    placed = (
        P("mesh", None, None, None),
        P("mesh", None),
        P(),
        P("mesh", "state"),
        P(("mesh", "state"), None),
        P("mesh", "state"),
    )
    return jax.shard_map(
        per_device,
        mesh=mesh,
        in_specs=placed,
        out_specs=(P(("mesh", "state"), None), P("mesh", "state")),
        check_vma=False,
    )
```

```python
import functools
import jax
import jax.numpy as jnp
from jax import lax
from jax.experimental import pallas as pl
from jax.experimental.pallas import tpu as pltpu
from jax.sharding import PartitionSpec as P

ITERS = 2
NEAR = 6
FAR = 2
LAG = 1
VMEM_LIMIT = 60 * 1024 * 1024
F32 = jnp.float32
BF16 = jnp.bfloat16


def vmem():
    return pl.BlockSpec(memory_space=pltpu.VMEM)


def smem():
    return pl.BlockSpec(memory_space=pltpu.SMEM)


def hbm():
    return pl.BlockSpec(memory_space=pl.ANY)


def far_plan(flat_cols, me, peers, rows):
    owners = flat_cols // rows
    places = flat_cols % rows
    delta = (owners - me + peers) % peers
    is_own = delta == 0
    is_left = delta == peers - 1
    is_right = delta == 1
    is_far = ~(is_own | is_left | is_right)
    ids = jnp.arange(peers * rows, dtype=jnp.int32)
    hits = (flat_cols[:, None] == ids[None, :]) & is_far[:, None]
    needed = jnp.max(hits.astype(jnp.int32), axis=0).reshape(peers, rows)
    before = jnp.arange(rows)[:, None] < jnp.arange(rows)[None, :]
    ranks = jnp.sum(needed[:, :, None] * before[None].astype(jnp.int32), axis=1)
    place_ids = jnp.arange(rows, dtype=jnp.int32)
    requests = jnp.stack(
        [jnp.sum(needed * (ranks == s) * place_ids[None, :], axis=1) for s in range(FAR)],
        axis=1,
    )
    slots = jnp.sum(hits.astype(jnp.int32) * ranks.reshape(1, -1), axis=1)
    far_at = rows + 2 * NEAR + (delta - 2) * FAR + slots
    sources = jnp.where(
        is_own,
        places,
        jnp.where(
            is_left,
            rows + places - (rows - NEAR),
            jnp.where(is_right, rows + NEAR + places, far_at),
        ),
    )
    return sources.astype(jnp.int32), requests.astype(jnp.int32)


def ordered_sums(keys, bins):
    count = keys.shape[0]
    ids = jnp.arange(count, dtype=jnp.int32)
    full = keys * count + ids
    rank = jnp.sum((full[None, :] < full[:, None]).astype(jnp.int32), axis=1)
    here = (rank[:, None] == ids[None, :]).astype(jnp.int32)
    perm = jnp.sum(here * ids[:, None], axis=0)
    bin_ids = jnp.arange(bins, dtype=jnp.int32)[:, None]
    upto = jnp.sum((keys[None, :] <= bin_ids).astype(jnp.int32), axis=1)
    some = jnp.any(keys[None, :] == bin_ids, axis=1)
    return perm, jnp.where(some, upto - 1, -1)


def solve_kernel(
    sweeps, peers, states,
    want_ref, src_ref, pair_perm, pair_last,
    start_hbm, kern_hbm, mix_hbm, mu_hbm, nu_hbm,
    u_ref, v_ref,
    kern, mix, mix_t, mu_t, u_t, table_0, table_1, blocks_0, blocks_1, outbox, products, sums,
    arrived_0, arrived_1, running, inbox, packed, asked, arr_key, arr_count,
    a_out, a_in, b_out, b_in,
    local_sem, near_send, near_recv, far_send, far_recv,
    back_near_send, back_near_recv, back_far_send, back_far_recv,
    a_send, a_recv, b_send, b_recv, ask_send, ask_recv,
):
    me = lax.axis_index("mesh")
    mz = lax.axis_index("state")
    rows, degree, size, _ = kern.shape
    table, blocks, arrived = (table_0, table_1), (blocks_0, blocks_1), (arrived_0, arrived_1)
    half = table_0.shape[1]
    per = rows // states
    far0 = rows + 2 * NEAR
    others = peers - 3
    right = lax.rem(me + 1, peers)
    left = lax.rem(me + peers - 1, peers)

    kern_copy = pltpu.make_async_copy(kern_hbm, kern, local_sem.at[0])
    mix_copy = pltpu.make_async_copy(mix_hbm, mix, local_sem.at[1])
    mu_copy = pltpu.make_async_copy(mu_hbm, u_ref, local_sem.at[3])
    nu_copy = pltpu.make_async_copy(nu_hbm, v_ref, local_sem.at[4])
    start_copy = pltpu.make_async_copy(start_hbm, v_ref, local_sem.at[5])
    start_copy.start()

    barrier = pltpu.get_barrier_semaphore()

    def greet(o, _):
        pl.semaphore_signal(barrier, inc=1, device_id={"mesh": lax.rem(me + o, peers)})
        return 0

    lax.fori_loop(1, peers, greet, 0)
    for j in range(1, states):
        pl.semaphore_signal(barrier, inc=1, device_id={"state": lax.rem(mz + j, states)})

    def ask(o):
        q = lax.rem(me + o, peers)
        return pltpu.make_async_remote_copy(
            src_ref=want_ref.at[q],
            dst_ref=inbox.at[peers - o - 1],
            send_sem=ask_send.at[o],
            recv_sem=ask_recv,
            device_id={"mesh": q},
        )

    def ask_start(o, _):
        ask(o).start()
        return 0

    def ask_sent(o, _):
        ask(o).wait_send()
        return 0

    pl.semaphore_wait(barrier, peers - 1 + states - 1)
    lax.fori_loop(1, peers, ask_start, 0)
    start_copy.wait()
    kern_copy.start()
    mix_copy.start()
    mu_copy.start()

    def cast(p, _):
        v = v_ref[p].astype(BF16).T
        for h in range(2):
            table[h][p] = v[h * half : (h + 1) * half]
            blocks[h][p] = v[h * half : (h + 1) * half]
        return 0

    lax.fori_loop(0, rows, cast, 0)
    pltpu.make_async_remote_copy(
        src_ref=inbox,
        dst_ref=inbox,
        send_sem=ask_send.at[0],
        recv_sem=ask_recv,
        device_id={"mesh": right},
    ).wait_recv()
    asked_copy = pltpu.make_async_copy(inbox, asked, local_sem.at[6])
    asked_copy.start()
    asked_copy.wait()

    def every(body):
        def one(i, _):
            body(2 + lax.rem(i * 12, others))
            return 0

        lax.fori_loop(0, others, one, 0)

    def fwd_near(h, k):
        return pltpu.make_async_remote_copy(
            src_ref=blocks[h].at[pl.ds((rows - NEAR, 0)[k], NEAR)],
            dst_ref=table[h].at[pl.ds(rows + k * NEAR, NEAR)],
            send_sem=near_send.at[h, k],
            recv_sem=near_recv.at[h, k],
            device_id={"mesh": (right, left)[k]},
        )

    def fwd_far(h, o):
        at = peers - o
        return pltpu.make_async_remote_copy(
            src_ref=outbox.at[h, pl.ds(2 * NEAR + (o - 2) * FAR, FAR)],
            dst_ref=table[h].at[pl.ds(far0 + (at - 2) * FAR, FAR)],
            send_sem=far_send.at[h],
            recv_sem=far_recv.at[h],
            device_id={"mesh": lax.rem(me + o, peers)},
        )

    def back_near(h, k):
        return pltpu.make_async_remote_copy(
            src_ref=outbox.at[h, pl.ds(k * NEAR, NEAR)],
            dst_ref=arrived[h].at[pl.ds(k * NEAR, NEAR)],
            send_sem=back_near_send.at[h, k],
            recv_sem=back_near_recv.at[h, k],
            device_id={"mesh": (left, right)[k]},
        )

    def back_far(h, o):
        at = peers - o
        return pltpu.make_async_remote_copy(
            src_ref=outbox.at[h, pl.ds(2 * NEAR + (o - 2) * FAR, FAR)],
            dst_ref=arrived[h].at[pl.ds(2 * NEAR + (at - 2) * FAR, FAR)],
            send_sem=back_far_send.at[h],
            recv_sem=back_far_recv.at[h],
            device_id={"mesh": lax.rem(me + o, peers)},
        )

    def a_copy(h, j, sub):
        to = lax.rem(mz + j, states)
        return pltpu.make_async_remote_copy(
            src_ref=a_out.at[h, to, sub],
            dst_ref=a_in.at[h, mz, sub],
            send_sem=a_send.at[h, j, sub],
            recv_sem=a_recv.at[h, j, sub],
            device_id={"state": to},
        )

    def b_copy(h, j, sub):
        to = lax.rem(mz + j, states)
        return pltpu.make_async_remote_copy(
            src_ref=b_out.at[h, to, sub],
            dst_ref=b_in.at[h, mz, sub],
            send_sem=b_send.at[h, j, sub],
            recv_sem=b_recv.at[h, j, sub],
            device_id={"state": to},
        )

    def all_far(h):
        return pltpu.make_async_remote_copy(
            src_ref=outbox.at[h, pl.ds(2 * NEAR, others * FAR)],
            dst_ref=table[h].at[pl.ds(far0, others * FAR)],
            send_sem=far_send.at[h],
            recv_sem=far_recv.at[h],
            device_id={"mesh": right},
        )

    def all_back(h):
        return pltpu.make_async_remote_copy(
            src_ref=outbox.at[h, pl.ds(2 * NEAR, others * FAR)],
            dst_ref=arrived[h].at[pl.ds(2 * NEAR, others * FAR)],
            send_sem=back_far_send.at[h],
            recv_sem=back_far_recv.at[h],
            device_id={"mesh": right},
        )

    def send_forward(h):
        for k in range(2):
            fwd_near(h, k).start()

        def send(o):
            for f in range(FAR):
                outbox[h, 2 * NEAR + (o - 2) * FAR + f] = blocks[h][asked[o - 1, 0, f]]
            fwd_far(h, o).start()

        every(send)

    def receive_forward(h):
        for k in range(2):
            fwd_near(h, k).wait_recv()
        all_far(h).wait_recv()

    def forward_sent(h):
        for k in range(2):
            fwd_near(h, k).wait_send()
        all_far(h).wait_send()

    def apply_rows(h, sub):
        for j in list(range(1, states)) + [0]:
            to = lax.rem(mz + j, states)
            r = to * per + sub
            lhs = jnp.concatenate(
                [table[h][src_ref[r * degree + k]] for k in range(degree)], axis=1
            )
            rhs = jnp.concatenate([kern[r, k] for k in range(degree)], axis=1)
            out = lax.dot_general(
                lhs, rhs, (((1,), (1,)), ((), ())), preferred_element_type=F32
            ).astype(BF16)
            if j == 0:
                a_in[h, mz, sub] = out
            else:
                a_out[h, to, sub] = out
                a_copy(h, j, sub).start()

    def mix_rows(t):
        for i in range(2):
            for h in range(2):
                for j in range(1, states):
                    a_copy(h, j, 2 * t + i).wait_recv()
        a = jnp.concatenate(
            [
                jnp.concatenate([a_in[h, z, 2 * t + i] for i in range(2)], axis=1)
                for z in range(states)
                for h in range(2)
            ],
            axis=0,
        )
        kv = jnp.dot(mix[...], a, preferred_element_type=F32)
        u = mu_t[t] / kv
        u_t[t] = u
        b = jnp.dot(mix_t[...], u.astype(BF16), preferred_element_type=F32).astype(BF16)
        for i in range(2):
            for z in range(states):
                for h in range(2):
                    b_out[h, z, 2 * t + i] = b[
                        (2 * z + h) * half : (2 * z + h + 1) * half, i * size : (i + 1) * size
                    ]
            for j in range(1, states):
                b_copy(0, j, 2 * t + i).start()
            for h in range(2):
                b_in[h, mz, 2 * t + i] = b_out[h, mz, 2 * t + i]

    def product_rows(h, sub):
        for j in range(1, states):
            b_copy(h, j, sub).wait_recv()
        for z in range(states):
            r = z * per + sub
            b = b_in[h, z, sub]
            for k in range(0, degree, 2):
                rhs = jnp.concatenate([kern[r, k], kern[r, k + 1]], axis=1)
                both = jnp.dot(b, rhs, preferred_element_type=F32)
                products[r * degree + k] = both[:, :size]
                products[r * degree + k + 1] = both[:, size:]

    def chain(t, _):
        steps = per // 2

        @pl.when(t < steps)
        def _():
            for i in range(2):
                apply_rows(1, 2 * t + i)

        @pl.when((t >= LAG) & (t < steps + LAG))
        def _():
            mix_rows(t - LAG)

        @pl.when(t == steps + LAG - 1)
        def _():
            def rest(sub, _):
                for j in range(1, states):
                    b_copy(1, j, sub).start()
                return 0

            lax.fori_loop(0, per, rest, 0)

        @pl.when(t >= 2 * LAG)
        def _():
            for i in range(2):
                product_rows(0, 2 * (t - 2 * LAG) + i)

        return 0

    def zeros():
        return jnp.zeros((half, size), F32)

    def pick(got, at):
        return jnp.where(at >= 0, got.astype(F32), zeros())

    def sum_products(h):
        def add(i, carry):
            acc, before = carry
            for g in range(8):
                p = pair_perm[i * 8 + g]
                now = src_ref[p]
                acc = jnp.where(now == before, acc, zeros()) + products[p]
                sums[h, i * 8 + g] = acc.astype(BF16)
                before = now
            return acc, before

        lax.fori_loop(0, rows * degree // 8, add, (zeros(), jnp.int32(-1)))

    def send_back(h):
        def load(i):
            at = pair_last[rows + i]
            got = sums[h, jnp.maximum(at, 0)]
            outbox[h, i] = jnp.where(at >= 0, got, jnp.zeros_like(got))

        def pack_near(i, _):
            load(i)
            return 0

        lax.fori_loop(0, 2 * NEAR, pack_near, 0)
        for k in range(2):
            back_near(h, k).start()

        def give(o):
            for f in range(FAR):
                load(2 * NEAR + (o - 2) * FAR + f)
            back_far(h, o).start()

        every(give)

    def receive_back(h):
        for k in range(2):
            back_near(h, k).wait_recv()
        all_back(h).wait_recv()
        for k in range(2):
            back_near(h, k).wait_send()
        all_back(h).wait_send()

    def finish_all(h):
        def add(i, carry):
            acc, before = carry
            e = lax.rem(arr_key[i], base)
            now = arr_key[i] // base
            acc = jnp.where(now == before, acc, zeros()) + arrived[h][2 * NEAR + e].astype(F32)
            running[i] = acc
            return acc, now

        lax.fori_loop(0, others * FAR, add, (zeros(), jnp.int32(-1)))

        def finish(p, near):
            at = pair_last[p]
            far = jnp.where(arr_count[p + 1] > arr_count[p], arr_count[p + 1] - 1, -1)
            total = pick(sums[h, jnp.maximum(at, 0)], at) + pick(running[jnp.maximum(far, 0)], far)
            if near is not None:
                total = total + arrived[h][near].astype(F32)
            v = v_ref[p, h * half : (h + 1) * half] / total
            v_ref[p, h * half : (h + 1) * half] = v
            rounded = v.astype(BF16)
            table[h][p] = rounded
            blocks[h][p] = rounded
            return 0

        lax.fori_loop(0, NEAR, lambda p, _: finish(p, NEAR + p), 0)
        lax.fori_loop(NEAR, rows - NEAR, lambda p, _: finish(p, None), 0)
        lax.fori_loop(rows - NEAR, rows, lambda p, _: finish(p, p - (rows - NEAR)), 0)

    for h in range(2):
        send_forward(h)
    lax.fori_loop(1, peers, ask_sent, 0)

    base = peers * FAR

    def order_arrivals():
        for q in range(peers - 1):
            packed[q, :] = inbox[q, 0, :]
        packed[peers - 1, :] = jnp.zeros((packed.shape[1],), jnp.int32)
        lane = lax.broadcasted_iota(jnp.int32, packed.shape, 1)
        ahead = lax.broadcasted_iota(jnp.int32, packed.shape, 0) + 1
        real = (lane < FAR) & (ahead >= 2) & (ahead <= peers - 2)
        beyond = rows * base
        keys = jnp.where(real, packed[...] * base + (ahead - 2) * FAR + lane, beyond)

        def next_key(i, last):
            key = jnp.min(jnp.where(keys > last, keys, beyond))
            arr_key[i] = key
            return key

        lax.fori_loop(0, others * FAR, next_key, jnp.int32(-1))
        arr_count[0] = 0

        def count(i, _):
            for g in range(4):
                p = i * 4 + g + 1
                arr_count[p] = jnp.sum((keys < p * base).astype(jnp.int32))
            return 0

        lax.fori_loop(0, rows // 4, count, 0)

    def sweep(s, _):
        nu_copy.start()

        @pl.when(s == 0)
        def _():
            mix_copy.wait()
            mu_copy.wait()
            for i in range(states):
                for j in range(states):
                    a, b = slice(i * size, (i + 1) * size), slice(j * size, (j + 1) * size)
                    mix_t[a, b] = mix[b, a].T

            def turn_mu(t, _):
                for i in range(2):
                    mu_t[t, :, i * size : (i + 1) * size] = u_ref[2 * t + i].T
                return 0

            lax.fori_loop(0, per // 2, turn_mu, 0)
            kern_copy.wait()

        nu_copy.wait()

        def turn_nu(p, _):
            v_ref[p] = v_ref[p].T
            return 0

        lax.fori_loop(0, rows, turn_nu, 0)

        receive_forward(0)
        lax.fori_loop(0, per, lambda sub, _: (apply_rows(0, sub), 0)[1], 0)

        @pl.when(s == 0)
        def _():
            order_arrivals()

        receive_forward(1)
        lax.fori_loop(0, per // 2 + 2 * LAG, chain, 0)
        for h in range(2):
            forward_sent(h)
        sum_products(0)
        send_back(0)
        lax.fori_loop(0, per, lambda sub, _: (product_rows(1, sub), 0)[1], 0)
        sum_products(1)
        send_back(1)

        def settle(sub, _):
            for h in range(2):
                for j in range(1, states):
                    a_copy(h, j, sub).wait_send()
                    b_copy(h, j, sub).wait_send()
            return 0

        lax.fori_loop(0, per, settle, 0)

        @pl.when(s == sweeps - 1)
        def _():
            def turn_u(t, _):
                for i in range(2):
                    u_ref[2 * t + i] = u_t[t, :, i * size : (i + 1) * size].T
                return 0

            lax.fori_loop(0, per // 2, turn_u, 0)

        for h in range(2):
            receive_back(h)
            finish_all(h)

            @pl.when(s < sweeps - 1)
            def _():
                send_forward(h)

        return 0

    lax.fori_loop(0, sweeps, sweep, 0)

    def turn_v(p, _):
        v_ref[p] = v_ref[p].T
        return 0

    lax.fori_loop(0, rows, turn_v, 0)


def per_device(kern_blocks, kern_cols, state_kernel, start_v, mu, nu):
    rows, degree, size, _ = kern_blocks.shape
    local_rows, cols = start_v.shape
    peers = lax.axis_size("mesh")
    states = lax.axis_size("state")
    me = lax.axis_index("mesh")
    per = rows // states
    nfar = (peers - 3) * FAR
    table_size = rows + 2 * NEAR + nfar
    nodes = states * cols
    dma = pltpu.SemaphoreType.DMA
    sources, requests = far_plan(kern_cols.reshape(-1), me, peers, rows)
    want = jnp.pad(requests, ((0, 0), (0, cols - FAR))).reshape(peers, 1, cols)
    pair_perm, pair_last = ordered_sums(sources, table_size)
    half = cols // 2

    def scratch(*dims, dtype=BF16):
        return pltpu.VMEM(dims + (half, size), dtype)

    potential_u, values = pl.pallas_call(
        functools.partial(solve_kernel, ITERS, peers, states),
        out_shape=(
            jax.ShapeDtypeStruct((per, size, nodes), F32),
            jax.ShapeDtypeStruct((rows, size, cols), F32),
        ),
        in_specs=[vmem()] + [smem()] * 3 + [hbm()] * 5,
        out_specs=(vmem(), vmem()),
        scratch_shapes=[
            pltpu.VMEM((rows, degree, size, size), BF16),
            pltpu.VMEM((nodes, nodes), BF16),
            pltpu.VMEM((nodes, nodes), BF16),
            pltpu.VMEM((per // 2, nodes, 2 * size), F32),
            pltpu.VMEM((per // 2, nodes, 2 * size), F32),
            scratch(table_size),
            scratch(table_size),
            scratch(rows),
            scratch(rows),
            scratch(2, 2 * NEAR + nfar),
            scratch(rows * degree, dtype=F32),
            scratch(2, rows * degree),
            scratch(2 * NEAR + nfar),
            scratch(2 * NEAR + nfar),
            scratch(nfar, dtype=F32),
            pltpu.VMEM((peers - 1, 1, cols), jnp.int32),
            pltpu.VMEM((peers, cols), jnp.int32),
            pltpu.SMEM((peers - 1, 1, cols), jnp.int32),
            pltpu.SMEM((nfar,), jnp.int32),
            pltpu.SMEM((rows + 1,), jnp.int32),
            scratch(2, states, per),
            scratch(2, states, per),
            scratch(2, states, per),
            scratch(2, states, per),
            dma((7,)),
            dma((2, 2)), dma((2, 2)), dma((2,)), dma((2,)),
            dma((2, 2)), dma((2, 2)), dma((2,)), dma((2,)),
            dma((2, states, per)), dma((2, states, per)),
            dma((2, states, per)), dma((2, states, per)),
            dma((peers,)), dma,
        ],
        compiler_params=pltpu.CompilerParams(
            vmem_limit_bytes=VMEM_LIMIT, collective_id=0, has_side_effects=True
        ),
        name="solve",
    )(
        want, sources, pair_perm, pair_last,
        start_v.reshape(rows, size, cols), kern_blocks, state_kernel,
        mu.reshape(per, size, nodes),
        nu.reshape(rows, size, cols),
    )
    return (
        potential_u.reshape(local_rows // states, nodes),
        values.reshape(local_rows, cols),
    )


def solution(mesh):
    placed = (
        P("mesh", None, None, None),
        P("mesh", None),
        P(),
        P("mesh", "state"),
        P(("mesh", "state"), None),
        P("mesh", "state"),
    )
    return jax.shard_map(
        per_device,
        mesh=mesh,
        in_specs=placed,
        out_specs=(P(("mesh", "state"), None), P("mesh", "state")),
        check_vma=False,
    )
```

```python
import functools
import jax
import jax.numpy as jnp
from jax import lax
from jax.experimental import pallas as pl
from jax.experimental.pallas import tpu as pltpu
from jax.sharding import PartitionSpec as P

ITERS = 2
NEAR = 6
FAR = 2
LAG = 1
VMEM_LIMIT = 60 * 1024 * 1024
F32 = jnp.float32
BF16 = jnp.bfloat16


def vmem():
    return pl.BlockSpec(memory_space=pltpu.VMEM)


def smem():
    return pl.BlockSpec(memory_space=pltpu.SMEM)


def hbm():
    return pl.BlockSpec(memory_space=pl.ANY)


def far_plan(flat_cols, me, peers, rows):
    owners = flat_cols // rows
    places = flat_cols % rows
    delta = (owners - me + peers) % peers
    is_own = delta == 0
    is_left = delta == peers - 1
    is_right = delta == 1
    is_far = ~(is_own | is_left | is_right)
    ids = jnp.arange(peers * rows, dtype=jnp.int32)
    hits = (flat_cols[:, None] == ids[None, :]) & is_far[:, None]
    needed = jnp.max(hits.astype(jnp.int32), axis=0).reshape(peers, rows)
    before = jnp.arange(rows)[:, None] < jnp.arange(rows)[None, :]
    ranks = jnp.sum(needed[:, :, None] * before[None].astype(jnp.int32), axis=1)
    place_ids = jnp.arange(rows, dtype=jnp.int32)
    requests = jnp.stack(
        [jnp.sum(needed * (ranks == s) * place_ids[None, :], axis=1) for s in range(FAR)],
        axis=1,
    )
    slots = jnp.sum(hits.astype(jnp.int32) * ranks.reshape(1, -1), axis=1)
    far_at = rows + 2 * NEAR + (delta - 2) * FAR + slots
    sources = jnp.where(
        is_own,
        places,
        jnp.where(
            is_left,
            rows + places - (rows - NEAR),
            jnp.where(is_right, rows + NEAR + places, far_at),
        ),
    )
    return sources.astype(jnp.int32), requests.astype(jnp.int32)


def ordered_sums(keys, bins):
    count = keys.shape[0]
    ids = jnp.arange(count, dtype=jnp.int32)
    full = keys * count + ids
    rank = jnp.sum((full[None, :] < full[:, None]).astype(jnp.int32), axis=1)
    here = (rank[:, None] == ids[None, :]).astype(jnp.int32)
    perm = jnp.sum(here * ids[:, None], axis=0)
    bin_ids = jnp.arange(bins, dtype=jnp.int32)[:, None]
    upto = jnp.sum((keys[None, :] <= bin_ids).astype(jnp.int32), axis=1)
    some = jnp.any(keys[None, :] == bin_ids, axis=1)
    return perm, jnp.where(some, upto - 1, -1)


def solve_kernel(
    sweeps, peers, states,
    want_ref, src_ref, pair_perm, pair_last,
    start_hbm, kern_hbm, mix_hbm, mu_hbm, nu_hbm,
    u_ref, v_ref,
    kern, mix, mix_t, mu_t, nu_t, u_t, table_0, table_1, blocks_0, blocks_1, outbox, products, sums,
    arrived_0, arrived_1, running, inbox, packed, asked, arr_key, arr_count,
    a_out, a_in, b_out, b_in,
    local_sem, near_send, near_recv, far_send, far_recv,
    back_near_send, back_near_recv, back_far_send, back_far_recv,
    a_send, a_recv, b_send, b_recv, c_send, c_recv, ask_send, ask_recv,
):
    me = lax.axis_index("mesh")
    mz = lax.axis_index("state")
    rows, degree, size, _ = kern.shape
    table, blocks, arrived = (table_0, table_1), (blocks_0, blocks_1), (arrived_0, arrived_1)
    half = table_0.shape[1]
    per = rows // states
    far0 = rows + 2 * NEAR
    others = peers - 3
    right = lax.rem(me + 1, peers)
    left = lax.rem(me + peers - 1, peers)

    kern_copy = pltpu.make_async_copy(kern_hbm, kern, local_sem.at[0])
    mix_copy = pltpu.make_async_copy(mix_hbm, mix, local_sem.at[1])
    mu_copy = pltpu.make_async_copy(mu_hbm, u_ref, local_sem.at[3])
    nu_copy = pltpu.make_async_copy(nu_hbm, v_ref, local_sem.at[4])
    start_copy = pltpu.make_async_copy(start_hbm, v_ref, local_sem.at[5])
    start_copy.start()

    barrier = pltpu.get_barrier_semaphore()

    def greet(o, _):
        pl.semaphore_signal(barrier, inc=1, device_id={"mesh": lax.rem(me + o, peers)})
        return 0

    lax.fori_loop(1, peers, greet, 0)
    for j in range(1, states):
        pl.semaphore_signal(barrier, inc=1, device_id={"state": lax.rem(mz + j, states)})

    def ask(o):
        q = lax.rem(me + o, peers)
        return pltpu.make_async_remote_copy(
            src_ref=want_ref.at[q],
            dst_ref=inbox.at[peers - o - 1],
            send_sem=ask_send.at[o],
            recv_sem=ask_recv,
            device_id={"mesh": q},
        )

    def ask_start(o, _):
        ask(o).start()
        return 0

    def ask_sent(o, _):
        ask(o).wait_send()
        return 0

    pl.semaphore_wait(barrier, peers - 1 + states - 1)
    lax.fori_loop(1, peers, ask_start, 0)
    start_copy.wait()
    kern_copy.start()
    mix_copy.start()
    mu_copy.start()

    def cast(p, _):
        v = v_ref[p].astype(BF16).T
        for h in range(2):
            table[h][p] = v[h * half : (h + 1) * half]
            blocks[h][p] = v[h * half : (h + 1) * half]
        return 0

    lax.fori_loop(0, rows, cast, 0)
    def every(body):
        def one(i, _):
            body(2 + lax.rem(i * 12, others))
            return 0

        lax.fori_loop(0, others, one, 0)

    def fwd_near(h, k):
        return pltpu.make_async_remote_copy(
            src_ref=blocks[h].at[pl.ds((rows - NEAR, 0)[k], NEAR)],
            dst_ref=table[h].at[pl.ds(rows + k * NEAR, NEAR)],
            send_sem=near_send.at[h, k],
            recv_sem=near_recv.at[h, k],
            device_id={"mesh": (right, left)[k]},
        )

    def fwd_far(h, o):
        at = peers - o
        return pltpu.make_async_remote_copy(
            src_ref=outbox.at[h, pl.ds(2 * NEAR + (o - 2) * FAR, FAR)],
            dst_ref=table[h].at[pl.ds(far0 + (at - 2) * FAR, FAR)],
            send_sem=far_send.at[h],
            recv_sem=far_recv.at[h],
            device_id={"mesh": lax.rem(me + o, peers)},
        )

    def back_near(h, k):
        return pltpu.make_async_remote_copy(
            src_ref=outbox.at[h, pl.ds(k * NEAR, NEAR)],
            dst_ref=arrived[h].at[pl.ds(k * NEAR, NEAR)],
            send_sem=back_near_send.at[h, k],
            recv_sem=back_near_recv.at[h, k],
            device_id={"mesh": (left, right)[k]},
        )

    def back_far(h, o):
        at = peers - o
        return pltpu.make_async_remote_copy(
            src_ref=outbox.at[h, pl.ds(2 * NEAR + (o - 2) * FAR, FAR)],
            dst_ref=arrived[h].at[pl.ds(2 * NEAR + (at - 2) * FAR, FAR)],
            send_sem=back_far_send.at[h],
            recv_sem=back_far_recv.at[h],
            device_id={"mesh": lax.rem(me + o, peers)},
        )

    def a_copy(h, j, t):
        to = lax.rem(mz + j, states)
        return pltpu.make_async_remote_copy(
            src_ref=a_out.at[h, to, pl.ds(2 * t, 2)],
            dst_ref=a_in.at[h, mz, pl.ds(2 * t, 2)],
            send_sem=a_send.at[h, j, t],
            recv_sem=a_recv.at[h, j, t],
            device_id={"state": to},
        )

    def b_copy(j, t):
        to = lax.rem(mz + j, states)
        return pltpu.make_async_remote_copy(
            src_ref=b_out.at[0, to, pl.ds(2 * t, 2)],
            dst_ref=b_in.at[0, mz, pl.ds(2 * t, 2)],
            send_sem=b_send.at[j, t],
            recv_sem=b_recv.at[j, t],
            device_id={"state": to},
        )

    def b_rest(j):
        to = lax.rem(mz + j, states)
        return pltpu.make_async_remote_copy(
            src_ref=b_out.at[1, to],
            dst_ref=b_in.at[1, mz],
            send_sem=c_send.at[j],
            recv_sem=c_recv.at[j],
            device_id={"state": to},
        )

    def all_far(h):
        return pltpu.make_async_remote_copy(
            src_ref=outbox.at[h, pl.ds(2 * NEAR, others * FAR)],
            dst_ref=table[h].at[pl.ds(far0, others * FAR)],
            send_sem=far_send.at[h],
            recv_sem=far_recv.at[h],
            device_id={"mesh": right},
        )

    def all_back(h):
        return pltpu.make_async_remote_copy(
            src_ref=outbox.at[h, pl.ds(2 * NEAR, others * FAR)],
            dst_ref=arrived[h].at[pl.ds(2 * NEAR, others * FAR)],
            send_sem=back_far_send.at[h],
            recv_sem=back_far_recv.at[h],
            device_id={"mesh": right},
        )

    def send_near(h):
        for k in range(2):
            fwd_near(h, k).start()

    def send_far(h):
        def send(o):
            for f in range(FAR):
                outbox[h, 2 * NEAR + (o - 2) * FAR + f] = blocks[h][asked[o - 1, 0, f]]
            fwd_far(h, o).start()

        every(send)

    def receive_forward(h):
        for k in range(2):
            fwd_near(h, k).wait_recv()
        all_far(h).wait_recv()

    def forward_sent(h):
        for k in range(2):
            fwd_near(h, k).wait_send()
        all_far(h).wait_send()

    def apply_rows(h, t):
        for j in list(range(1, states)) + [0]:
            to = lax.rem(mz + j, states)
            for i in range(2):
                sub = 2 * t + i
                r = to * per + sub
                lhs = jnp.concatenate(
                    [table[h][src_ref[r * degree + k]] for k in range(degree)], axis=1
                )
                rhs = jnp.concatenate([kern[r, k] for k in range(degree)], axis=1)
                out = lax.dot_general(
                    lhs, rhs, (((1,), (1,)), ((), ())), preferred_element_type=F32
                ).astype(BF16)
                if j == 0:
                    a_in[h, mz, sub] = out
                else:
                    a_out[h, to, sub] = out
            if j > 0:
                a_copy(h, j, t).start()

    def mix_rows(t):
        for h in range(2):
            for j in range(1, states):
                a_copy(h, j, t).wait_recv()
        a = jnp.concatenate(
            [
                jnp.concatenate([a_in[h, z, 2 * t + i] for i in range(2)], axis=1)
                for z in range(states)
                for h in range(2)
            ],
            axis=0,
        )
        kv = jnp.dot(mix[...], a, preferred_element_type=F32)
        u = mu_t[t] / kv
        u_t[t] = u
        b = jnp.dot(mix_t[...], u.astype(BF16), preferred_element_type=F32).astype(BF16)
        for i in range(2):
            for z in range(states):
                for h in range(2):
                    b_out[h, z, 2 * t + i] = b[
                        (2 * z + h) * half : (2 * z + h + 1) * half, i * size : (i + 1) * size
                    ]
        for j in range(1, states):
            b_copy(j, t).start()
        for i in range(2):
            for h in range(2):
                b_in[h, mz, 2 * t + i] = b_out[h, mz, 2 * t + i]

    def product_rows(h, sub):
        for z in range(states):
            r = z * per + sub
            b = b_in[h, z, sub]
            for k in range(0, degree, 2):
                rhs = jnp.concatenate([kern[r, k], kern[r, k + 1]], axis=1)
                both = jnp.dot(b, rhs, preferred_element_type=F32)
                products[r * degree + k] = both[:, :size]
                products[r * degree + k + 1] = both[:, size:]

    def chain(t, _):
        steps = per // 2

        @pl.when(t < steps)
        def _():
            apply_rows(1, t)

        @pl.when((t >= LAG) & (t < steps + LAG))
        def _():
            mix_rows(t - LAG)

        @pl.when(t == steps + LAG - 1)
        def _():
            for j in range(1, states):
                b_rest(j).start()

        @pl.when(t >= 2 * LAG)
        def _():
            for j in range(1, states):
                b_copy(j, t - 2 * LAG).wait_recv()
            for i in range(2):
                product_rows(0, 2 * (t - 2 * LAG) + i)

        return 0

    def zeros():
        return jnp.zeros((half, size), F32)

    def pick(got, at):
        return jnp.where(at >= 0, got.astype(F32), zeros())

    def sum_products(h):
        def add(i, carry):
            acc, before = carry
            for g in range(8):
                p = pair_perm[i * 8 + g]
                now = src_ref[p]
                acc = jnp.where(now == before, acc, zeros()) + products[p]
                sums[h, i * 8 + g] = acc.astype(BF16)
                before = now
            return acc, before

        lax.fori_loop(0, rows * degree // 8, add, (zeros(), jnp.int32(-1)))

    def send_back(h):
        def load(i):
            at = pair_last[rows + i]
            got = sums[h, jnp.maximum(at, 0)]
            outbox[h, i] = jnp.where(at >= 0, got, jnp.zeros_like(got))

        def pack_near(i, _):
            load(i)
            return 0

        lax.fori_loop(0, 2 * NEAR, pack_near, 0)
        for k in range(2):
            back_near(h, k).start()

        def give(o):
            for f in range(FAR):
                load(2 * NEAR + (o - 2) * FAR + f)
            back_far(h, o).start()

        every(give)

    def receive_back(h):
        for k in range(2):
            back_near(h, k).wait_recv()
        all_back(h).wait_recv()
        for k in range(2):
            back_near(h, k).wait_send()
        all_back(h).wait_send()

    def finish_all(h, ending):
        def add(i, carry):
            acc, before = carry
            e = lax.rem(arr_key[i], base)
            now = arr_key[i] // base
            acc = jnp.where(now == before, acc, zeros()) + arrived[h][2 * NEAR + e].astype(F32)
            running[i] = acc
            return acc, now

        lax.fori_loop(0, others * FAR, add, (zeros(), jnp.int32(-1)))

        def finish(p, near):
            at = pair_last[p]
            far = jnp.where(arr_count[p + 1] > arr_count[p], arr_count[p + 1] - 1, -1)
            total = pick(sums[h, jnp.maximum(at, 0)], at) + pick(running[jnp.maximum(far, 0)], far)
            if near is not None:
                total = total + arrived[h][near].astype(F32)
            v = nu_t[p, h * half : (h + 1) * half] / total
            if ending:
                v_ref[p, :, h * half : (h + 1) * half] = v.T
            else:
                rounded = v.astype(BF16)
                table[h][p] = rounded
                blocks[h][p] = rounded
            return 0

        lax.fori_loop(0, NEAR, lambda p, _: finish(p, NEAR + p), 0)
        lax.fori_loop(NEAR, rows - NEAR, lambda p, _: finish(p, None), 0)
        lax.fori_loop(rows - NEAR, rows, lambda p, _: finish(p, p - (rows - NEAR)), 0)

    for h in range(2):
        send_near(h)
    pltpu.make_async_remote_copy(
        src_ref=inbox,
        dst_ref=inbox,
        send_sem=ask_send.at[0],
        recv_sem=ask_recv,
        device_id={"mesh": right},
    ).wait_recv()
    asked_copy = pltpu.make_async_copy(inbox, asked, local_sem.at[6])
    asked_copy.start()
    asked_copy.wait()
    for h in range(2):
        send_far(h)
    lax.fori_loop(1, peers, ask_sent, 0)

    base = peers * FAR

    def order_arrivals():
        for q in range(peers - 1):
            packed[q, :] = inbox[q, 0, :]
        packed[peers - 1, :] = jnp.zeros((packed.shape[1],), jnp.int32)
        lane = lax.broadcasted_iota(jnp.int32, packed.shape, 1)
        ahead = lax.broadcasted_iota(jnp.int32, packed.shape, 0) + 1
        real = (lane < FAR) & (ahead >= 2) & (ahead <= peers - 2)
        beyond = rows * base
        keys = jnp.where(real, packed[...] * base + (ahead - 2) * FAR + lane, beyond)

        def next_key(i, last):
            key = jnp.min(jnp.where(keys > last, keys, beyond))
            arr_key[i] = key
            return key

        lax.fori_loop(0, others * FAR, next_key, jnp.int32(-1))
        arr_count[0] = 0

        def count(i, _):
            for g in range(4):
                p = i * 4 + g + 1
                arr_count[p] = jnp.sum((keys < p * base).astype(jnp.int32))
            return 0

        lax.fori_loop(0, rows // 4, count, 0)

    def sweep(s, _):
        @pl.when(s == 0)
        def _():
            nu_copy.start()
            mix_copy.wait()
            mu_copy.wait()
            for i in range(states):
                for j in range(states):
                    a, b = slice(i * size, (i + 1) * size), slice(j * size, (j + 1) * size)
                    mix_t[a, b] = mix[b, a].T

            def turn_mu(t, _):
                for i in range(2):
                    mu_t[t, :, i * size : (i + 1) * size] = u_ref[2 * t + i].T
                return 0

            lax.fori_loop(0, per // 2, turn_mu, 0)
            nu_copy.wait()

            def turn_nu(p, _):
                nu_t[p] = v_ref[p].T
                return 0

            lax.fori_loop(0, rows, turn_nu, 0)
            kern_copy.wait()

        receive_forward(0)
        lax.fori_loop(0, per // 2, lambda t, _: (apply_rows(0, t), 0)[1], 0)

        @pl.when(s == 0)
        def _():
            order_arrivals()

        receive_forward(1)
        lax.fori_loop(0, per // 2 + 2 * LAG, chain, 0)
        for h in range(2):
            forward_sent(h)
        sum_products(0)
        send_back(0)
        for j in range(1, states):
            b_rest(j).wait_recv()
        lax.fori_loop(0, per, lambda sub, _: (product_rows(1, sub), 0)[1], 0)
        sum_products(1)
        send_back(1)

        for j in range(1, states):
            for t in range(per // 2):
                for h in range(2):
                    a_copy(h, j, t).wait_send()
                b_copy(j, t).wait_send()
            b_rest(j).wait_send()

        @pl.when(s == sweeps - 1)
        def _():
            def turn_u(t, _):
                for i in range(2):
                    u_ref[2 * t + i] = u_t[t, :, i * size : (i + 1) * size].T
                return 0

            lax.fori_loop(0, per // 2, turn_u, 0)

        for h in range(2):
            receive_back(h)

            @pl.when(s == sweeps - 1)
            def _():
                finish_all(h, True)

            @pl.when(s < sweeps - 1)
            def _():
                finish_all(h, False)
                send_near(h)
                send_far(h)

        return 0

    lax.fori_loop(0, sweeps, sweep, 0)


def per_device(kern_blocks, kern_cols, state_kernel, start_v, mu, nu):
    rows, degree, size, _ = kern_blocks.shape
    local_rows, cols = start_v.shape
    peers = lax.axis_size("mesh")
    states = lax.axis_size("state")
    me = lax.axis_index("mesh")
    per = rows // states
    nfar = (peers - 3) * FAR
    table_size = rows + 2 * NEAR + nfar
    nodes = states * cols
    dma = pltpu.SemaphoreType.DMA
    sources, requests = far_plan(kern_cols.reshape(-1), me, peers, rows)
    want = jnp.pad(requests, ((0, 0), (0, cols - FAR))).reshape(peers, 1, cols)
    pair_perm, pair_last = ordered_sums(sources, table_size)
    half = cols // 2

    def scratch(*dims, dtype=BF16):
        return pltpu.VMEM(dims + (half, size), dtype)

    potential_u, values = pl.pallas_call(
        functools.partial(solve_kernel, ITERS, peers, states),
        out_shape=(
            jax.ShapeDtypeStruct((per, size, nodes), F32),
            jax.ShapeDtypeStruct((rows, size, cols), F32),
        ),
        in_specs=[vmem()] + [smem()] * 3 + [hbm()] * 5,
        out_specs=(vmem(), vmem()),
        scratch_shapes=[
            pltpu.VMEM((rows, degree, size, size), BF16),
            pltpu.VMEM((nodes, nodes), BF16),
            pltpu.VMEM((nodes, nodes), BF16),
            pltpu.VMEM((per // 2, nodes, 2 * size), F32),
            pltpu.VMEM((rows, cols, size), F32),
            pltpu.VMEM((per // 2, nodes, 2 * size), F32),
            scratch(table_size),
            scratch(table_size),
            scratch(rows),
            scratch(rows),
            scratch(2, 2 * NEAR + nfar),
            scratch(rows * degree, dtype=F32),
            scratch(2, rows * degree),
            scratch(2 * NEAR + nfar),
            scratch(2 * NEAR + nfar),
            scratch(nfar, dtype=F32),
            pltpu.VMEM((peers - 1, 1, cols), jnp.int32),
            pltpu.VMEM((peers, cols), jnp.int32),
            pltpu.SMEM((peers - 1, 1, cols), jnp.int32),
            pltpu.SMEM((nfar,), jnp.int32),
            pltpu.SMEM((rows + 1,), jnp.int32),
            scratch(2, states, per),
            scratch(2, states, per),
            scratch(2, states, per),
            scratch(2, states, per),
            dma((7,)),
            dma((2, 2)), dma((2, 2)), dma((2,)), dma((2,)),
            dma((2, 2)), dma((2, 2)), dma((2,)), dma((2,)),
            dma((2, states, per // 2)), dma((2, states, per // 2)),
            dma((states, per // 2)), dma((states, per // 2)),
            dma((states,)), dma((states,)),
            dma((peers,)), dma,
        ],
        compiler_params=pltpu.CompilerParams(
            vmem_limit_bytes=VMEM_LIMIT, collective_id=0, has_side_effects=True
        ),
        name="solve",
    )(
        want, sources, pair_perm, pair_last,
        start_v.reshape(rows, size, cols), kern_blocks, state_kernel,
        mu.reshape(per, size, nodes),
        nu.reshape(rows, size, cols),
    )
    return (
        potential_u.reshape(local_rows // states, nodes),
        values.reshape(local_rows, cols),
    )


def solution(mesh):
    placed = (
        P("mesh", None, None, None),
        P("mesh", None),
        P(),
        P("mesh", "state"),
        P(("mesh", "state"), None),
        P("mesh", "state"),
    )
    return jax.shard_map(
        per_device,
        mesh=mesh,
        in_specs=placed,
        out_specs=(P(("mesh", "state"), None), P("mesh", "state")),
        check_vma=False,
    )
```

```python
import functools
import jax
import jax.numpy as jnp
from jax import lax
from jax.experimental import pallas as pl
from jax.experimental.pallas import tpu as pltpu
from jax.sharding import PartitionSpec as P

ITERS = 2
NEAR = 6
FAR = 2
LAG = 1
VMEM_LIMIT = 60 * 1024 * 1024
F32 = jnp.float32
BF16 = jnp.bfloat16


def vmem():
    return pl.BlockSpec(memory_space=pltpu.VMEM)


def smem():
    return pl.BlockSpec(memory_space=pltpu.SMEM)


def hbm():
    return pl.BlockSpec(memory_space=pl.ANY)


def far_plan(flat_cols, me, peers, rows):
    owners = flat_cols // rows
    places = flat_cols % rows
    delta = (owners - me + peers) % peers
    is_own = delta == 0
    is_left = delta == peers - 1
    is_right = delta == 1
    is_far = ~(is_own | is_left | is_right)
    ids = jnp.arange(peers * rows, dtype=jnp.int32)
    hits = (flat_cols[:, None] == ids[None, :]) & is_far[:, None]
    needed = jnp.max(hits.astype(jnp.int32), axis=0).reshape(peers, rows)
    before = jnp.arange(rows)[:, None] < jnp.arange(rows)[None, :]
    ranks = jnp.sum(needed[:, :, None] * before[None].astype(jnp.int32), axis=1)
    place_ids = jnp.arange(rows, dtype=jnp.int32)
    requests = jnp.stack(
        [jnp.sum(needed * (ranks == s) * place_ids[None, :], axis=1) for s in range(FAR)],
        axis=1,
    )
    slots = jnp.sum(hits.astype(jnp.int32) * ranks.reshape(1, -1), axis=1)
    far_at = rows + 2 * NEAR + (delta - 2) * FAR + slots
    sources = jnp.where(
        is_own,
        places,
        jnp.where(
            is_left,
            rows + places - (rows - NEAR),
            jnp.where(is_right, rows + NEAR + places, far_at),
        ),
    )
    return sources.astype(jnp.int32), requests.astype(jnp.int32)


def ordered_sums(keys, bins):
    count = keys.shape[0]
    ids = jnp.arange(count, dtype=jnp.int32)
    full = keys * count + ids
    rank = jnp.sum((full[None, :] < full[:, None]).astype(jnp.int32), axis=1)
    here = (rank[:, None] == ids[None, :]).astype(jnp.int32)
    perm = jnp.sum(here * ids[:, None], axis=0)
    bin_ids = jnp.arange(bins, dtype=jnp.int32)[:, None]
    upto = jnp.sum((keys[None, :] <= bin_ids).astype(jnp.int32), axis=1)
    some = jnp.any(keys[None, :] == bin_ids, axis=1)
    return perm, jnp.where(some, upto - 1, -1)


def solve_kernel(
    sweeps, peers, states,
    want_ref, src_ref, pair_perm, pair_last,
    start_hbm, kern_hbm, mix_hbm, mu_hbm, nu_hbm,
    u_ref, v_ref,
    kern, mix, mix_t, mu_t, nu_t, u_t, table_0, table_1, blocks_0, blocks_1, outbox, products, sums,
    arrived_0, arrived_1, running, inbox, packed, asked, arr_key, arr_count,
    a_out, a_in, b_out, b_in,
    local_sem, near_send, near_recv, far_send, far_recv,
    back_near_send, back_near_recv, back_far_send, back_far_recv,
    a_send, a_recv, b_send, b_recv, c_send, c_recv, ask_send, ask_recv,
):
    me = lax.axis_index("mesh")
    mz = lax.axis_index("state")
    rows, degree, size, _ = kern.shape
    table, blocks, arrived = (table_0, table_1), (blocks_0, blocks_1), (arrived_0, arrived_1)
    half = table_0.shape[1]
    per = rows // states
    far0 = rows + 2 * NEAR
    others = peers - 3
    right = lax.rem(me + 1, peers)
    left = lax.rem(me + peers - 1, peers)

    kern_copy = pltpu.make_async_copy(kern_hbm, kern, local_sem.at[0])
    mix_copy = pltpu.make_async_copy(mix_hbm, mix, local_sem.at[1])
    mu_copy = pltpu.make_async_copy(mu_hbm, u_ref, local_sem.at[3])
    nu_copy = pltpu.make_async_copy(nu_hbm, v_ref, local_sem.at[4])
    start_copy = pltpu.make_async_copy(start_hbm, v_ref, local_sem.at[5])
    start_copy.start()

    barrier = pltpu.get_barrier_semaphore()

    def greet(o, _):
        pl.semaphore_signal(barrier, inc=1, device_id={"mesh": lax.rem(me + o, peers)})
        return 0

    lax.fori_loop(1, peers, greet, 0)
    for j in range(1, states):
        pl.semaphore_signal(barrier, inc=1, device_id={"state": lax.rem(mz + j, states)})

    def ask(o):
        q = lax.rem(me + o, peers)
        return pltpu.make_async_remote_copy(
            src_ref=want_ref.at[q],
            dst_ref=inbox.at[peers - o - 1],
            send_sem=ask_send.at[o],
            recv_sem=ask_recv,
            device_id={"mesh": q},
        )

    def ask_start(o, _):
        ask(o).start()
        return 0

    def ask_sent(o, _):
        ask(o).wait_send()
        return 0

    pl.semaphore_wait(barrier, peers - 1 + states - 1)
    lax.fori_loop(1, peers, ask_start, 0)
    start_copy.wait()
    kern_copy.start()
    mix_copy.start()
    mu_copy.start()

    def cast(p, _):
        v = v_ref[p].astype(BF16).T
        for h in range(2):
            table[h][p] = v[h * half : (h + 1) * half]
            blocks[h][p] = v[h * half : (h + 1) * half]
        return 0

    lax.fori_loop(0, rows, cast, 0)
    def every(body):
        def one(i, _):
            body(2 + lax.rem(i * 12, others))
            return 0

        lax.fori_loop(0, others, one, 0)

    def fwd_near(h, k):
        return pltpu.make_async_remote_copy(
            src_ref=blocks[h].at[pl.ds((rows - NEAR, 0)[k], NEAR)],
            dst_ref=table[h].at[pl.ds(rows + k * NEAR, NEAR)],
            send_sem=near_send.at[h, k],
            recv_sem=near_recv.at[h, k],
            device_id={"mesh": (right, left)[k]},
        )

    def fwd_far(h, o):
        at = peers - o
        return pltpu.make_async_remote_copy(
            src_ref=outbox.at[h, pl.ds(2 * NEAR + (o - 2) * FAR, FAR)],
            dst_ref=table[h].at[pl.ds(far0 + (at - 2) * FAR, FAR)],
            send_sem=far_send.at[h],
            recv_sem=far_recv.at[h],
            device_id={"mesh": lax.rem(me + o, peers)},
        )

    def back_near(h, k):
        return pltpu.make_async_remote_copy(
            src_ref=outbox.at[h, pl.ds(k * NEAR, NEAR)],
            dst_ref=arrived[h].at[pl.ds(k * NEAR, NEAR)],
            send_sem=back_near_send.at[h, k],
            recv_sem=back_near_recv.at[h, k],
            device_id={"mesh": (left, right)[k]},
        )

    def back_far(h, o):
        at = peers - o
        return pltpu.make_async_remote_copy(
            src_ref=outbox.at[h, pl.ds(2 * NEAR + (o - 2) * FAR, FAR)],
            dst_ref=arrived[h].at[pl.ds(2 * NEAR + (at - 2) * FAR, FAR)],
            send_sem=back_far_send.at[h],
            recv_sem=back_far_recv.at[h],
            device_id={"mesh": lax.rem(me + o, peers)},
        )

    def a_copy(h, j, t):
        to = lax.rem(mz + j, states)
        return pltpu.make_async_remote_copy(
            src_ref=a_out.at[h, to, pl.ds(2 * t, 2)],
            dst_ref=a_in.at[h, mz, pl.ds(2 * t, 2)],
            send_sem=a_send.at[h, j, t],
            recv_sem=a_recv.at[h, j, t],
            device_id={"state": to},
        )

    def b_copy(j, t):
        to = lax.rem(mz + j, states)
        return pltpu.make_async_remote_copy(
            src_ref=b_out.at[0, to, pl.ds(2 * t, 2)],
            dst_ref=b_in.at[0, mz, pl.ds(2 * t, 2)],
            send_sem=b_send.at[j, t],
            recv_sem=b_recv.at[j, t],
            device_id={"state": to},
        )

    def b_rest(j):
        to = lax.rem(mz + j, states)
        return pltpu.make_async_remote_copy(
            src_ref=b_out.at[1, to],
            dst_ref=b_in.at[1, mz],
            send_sem=c_send.at[j],
            recv_sem=c_recv.at[j],
            device_id={"state": to},
        )

    def all_far(h):
        return pltpu.make_async_remote_copy(
            src_ref=outbox.at[h, pl.ds(2 * NEAR, others * FAR)],
            dst_ref=table[h].at[pl.ds(far0, others * FAR)],
            send_sem=far_send.at[h],
            recv_sem=far_recv.at[h],
            device_id={"mesh": right},
        )

    def all_back(h):
        return pltpu.make_async_remote_copy(
            src_ref=outbox.at[h, pl.ds(2 * NEAR, others * FAR)],
            dst_ref=arrived[h].at[pl.ds(2 * NEAR, others * FAR)],
            send_sem=back_far_send.at[h],
            recv_sem=back_far_recv.at[h],
            device_id={"mesh": right},
        )

    def send_near(h):
        for k in range(2):
            fwd_near(h, k).start()

    def send_far(h):
        def send(o):
            for f in range(FAR):
                outbox[h, 2 * NEAR + (o - 2) * FAR + f] = blocks[h][asked[o - 1, 0, f]]
            fwd_far(h, o).start()

        every(send)

    def receive_forward(h):
        for k in range(2):
            fwd_near(h, k).wait_recv()
        all_far(h).wait_recv()

    def forward_sent(h):
        for k in range(2):
            fwd_near(h, k).wait_send()
        all_far(h).wait_send()

    def apply_rows(h, t):
        for j in list(range(1, states)) + [0]:
            to = lax.rem(mz + j, states)
            for i in range(2):
                sub = 2 * t + i
                r = to * per + sub
                lhs = jnp.concatenate(
                    [table[h][src_ref[r * degree + k]] for k in range(degree)], axis=1
                )
                rhs = jnp.concatenate([kern[r, k] for k in range(degree)], axis=1)
                out = lax.dot_general(
                    lhs, rhs, (((1,), (1,)), ((), ())), preferred_element_type=F32
                ).astype(BF16)
                if j == 0:
                    a_in[h, mz, sub] = out
                else:
                    a_out[h, to, sub] = out
            if j > 0:
                a_copy(h, j, t).start()

    def mix_half(h, t):
        for j in range(1, states):
            a_copy(h, j, t).wait_recv()
        a = jnp.concatenate(
            [
                jnp.concatenate([a_in[h, z, 2 * t + i] for i in range(2)], axis=1)
                for z in range(states)
            ],
            axis=0,
        )
        wide = states * half
        return jnp.dot(mix[:, h * wide : (h + 1) * wide], a, preferred_element_type=F32)

    def mix_first(t, _):
        u_t[t] = mix_half(0, t)
        return 0

    def mix_rows(t):
        kv = u_t[t] + mix_half(1, t)
        u = mu_t[t] / kv
        u_t[t] = u
        b = jnp.dot(mix_t[...], u.astype(BF16), preferred_element_type=F32).astype(BF16)
        for i in range(2):
            for z in range(states):
                for h in range(2):
                    b_out[h, z, 2 * t + i] = b[
                        (2 * z + h) * half : (2 * z + h + 1) * half, i * size : (i + 1) * size
                    ]
        for j in range(1, states):
            b_copy(j, t).start()
        for i in range(2):
            for h in range(2):
                b_in[h, mz, 2 * t + i] = b_out[h, mz, 2 * t + i]

    def product_rows(h, sub):
        for z in range(states):
            r = z * per + sub
            b = b_in[h, z, sub]
            for k in range(0, degree, 2):
                rhs = jnp.concatenate([kern[r, k], kern[r, k + 1]], axis=1)
                both = jnp.dot(b, rhs, preferred_element_type=F32)
                products[r * degree + k] = both[:, :size]
                products[r * degree + k + 1] = both[:, size:]

    def chain(t, _):
        steps = per // 2

        @pl.when(t < steps)
        def _():
            apply_rows(1, t)

        @pl.when((t >= LAG) & (t < steps + LAG))
        def _():
            mix_rows(t - LAG)

        @pl.when(t == steps + LAG - 1)
        def _():
            for j in range(1, states):
                b_rest(j).start()

        @pl.when(t >= 2 * LAG)
        def _():
            for j in range(1, states):
                b_copy(j, t - 2 * LAG).wait_recv()
            for i in range(2):
                product_rows(0, 2 * (t - 2 * LAG) + i)

        return 0

    def zeros():
        return jnp.zeros((half, size), F32)

    def pick(got, at):
        return jnp.where(at >= 0, got.astype(F32), zeros())

    def sum_products(h):
        def add(i, carry):
            acc, before = carry
            for g in range(16):
                p = pair_perm[i * 16 + g]
                now = src_ref[p]
                acc = jnp.where(now == before, acc, zeros()) + products[p]
                sums[h, i * 16 + g] = acc.astype(BF16)
                before = now
            return acc, before

        lax.fori_loop(0, rows * degree // 16, add, (zeros(), jnp.int32(-1)))

    def send_back(h):
        def load(i):
            at = pair_last[rows + i]
            got = sums[h, jnp.maximum(at, 0)]
            outbox[h, i] = jnp.where(at >= 0, got, jnp.zeros_like(got))

        def pack_near(i, _):
            load(i)
            return 0

        lax.fori_loop(0, 2 * NEAR, pack_near, 0)
        for k in range(2):
            back_near(h, k).start()

        def give(o):
            for f in range(FAR):
                load(2 * NEAR + (o - 2) * FAR + f)
            back_far(h, o).start()

        every(give)

    def receive_back(h):
        for k in range(2):
            back_near(h, k).wait_recv()
        all_back(h).wait_recv()
        for k in range(2):
            back_near(h, k).wait_send()
        all_back(h).wait_send()

    def finish_all(h, ending):
        def add(i, carry):
            acc, before = carry
            e = lax.rem(arr_key[i], base)
            now = arr_key[i] // base
            acc = jnp.where(now == before, acc, zeros()) + arrived[h][2 * NEAR + e].astype(F32)
            running[i] = acc
            return acc, now

        lax.fori_loop(0, others * FAR, add, (zeros(), jnp.int32(-1)))

        def finish(p, near):
            at = pair_last[p]
            far = jnp.where(arr_count[p + 1] > arr_count[p], arr_count[p + 1] - 1, -1)
            total = pick(sums[h, jnp.maximum(at, 0)], at) + pick(running[jnp.maximum(far, 0)], far)
            if near is not None:
                total = total + arrived[h][near].astype(F32)
            v = nu_t[p, h * half : (h + 1) * half] / total
            if ending:
                v_ref[p, :, h * half : (h + 1) * half] = v.T
            else:
                rounded = v.astype(BF16)
                table[h][p] = rounded
                blocks[h][p] = rounded
            return 0

        lax.fori_loop(0, NEAR, lambda p, _: finish(p, NEAR + p), 0)
        lax.fori_loop(NEAR, rows - NEAR, lambda p, _: finish(p, None), 0)
        lax.fori_loop(rows - NEAR, rows, lambda p, _: finish(p, p - (rows - NEAR)), 0)

    for h in range(2):
        send_near(h)
    pltpu.make_async_remote_copy(
        src_ref=inbox,
        dst_ref=inbox,
        send_sem=ask_send.at[0],
        recv_sem=ask_recv,
        device_id={"mesh": right},
    ).wait_recv()
    asked_copy = pltpu.make_async_copy(inbox, asked, local_sem.at[6])
    asked_copy.start()
    asked_copy.wait()
    for h in range(2):
        send_far(h)
    lax.fori_loop(1, peers, ask_sent, 0)

    base = peers * FAR

    def order_arrivals():
        for q in range(peers - 1):
            packed[q, :] = inbox[q, 0, :]
        packed[peers - 1, :] = jnp.zeros((packed.shape[1],), jnp.int32)
        lane = lax.broadcasted_iota(jnp.int32, packed.shape, 1)
        ahead = lax.broadcasted_iota(jnp.int32, packed.shape, 0) + 1
        real = (lane < FAR) & (ahead >= 2) & (ahead <= peers - 2)
        beyond = rows * base
        keys = jnp.where(real, packed[...] * base + (ahead - 2) * FAR + lane, beyond)

        def next_key(i, last):
            key = jnp.min(jnp.where(keys > last, keys, beyond))
            arr_key[i] = key
            return key

        lax.fori_loop(0, others * FAR, next_key, jnp.int32(-1))
        arr_count[0] = 0

        def count(i, _):
            for g in range(4):
                p = i * 4 + g + 1
                arr_count[p] = jnp.sum((keys < p * base).astype(jnp.int32))
            return 0

        lax.fori_loop(0, rows // 4, count, 0)

    def sweep(s, _):
        @pl.when(s == 0)
        def _():
            nu_copy.start()
            mix_copy.wait()
            mu_copy.wait()
            for i in range(states):
                for j in range(states):
                    a, b = slice(i * size, (i + 1) * size), slice(j * size, (j + 1) * size)
                    mix_t[a, b] = mix[b, a].T
            for h in range(2):
                for z in range(0, states, 2):
                    two = [mix_t[(2 * (z + i) + h) * half : (2 * (z + i) + h + 1) * half] for i in range(2)]
                    at = (h * states + z) * half
                    mix[:, at : at + 2 * half] = jnp.concatenate(two, axis=0).T

            def turn_mu(t, _):
                for i in range(2):
                    mu_t[t, :, i * size : (i + 1) * size] = u_ref[2 * t + i].T
                return 0

            lax.fori_loop(0, per // 2, turn_mu, 0)
            nu_copy.wait()

            def turn_nu(p, _):
                nu_t[p] = v_ref[p].T
                return 0

            lax.fori_loop(0, rows, turn_nu, 0)
            kern_copy.wait()

        receive_forward(0)
        lax.fori_loop(0, per // 2, lambda t, _: (apply_rows(0, t), 0)[1], 0)

        @pl.when(s == 0)
        def _():
            order_arrivals()

        lax.fori_loop(0, per // 2, mix_first, 0)
        receive_forward(1)
        lax.fori_loop(0, per // 2 + 2 * LAG, chain, 0)
        for h in range(2):
            forward_sent(h)
        sum_products(0)
        send_back(0)
        for j in range(1, states):
            b_rest(j).wait_recv()
        lax.fori_loop(0, per, lambda sub, _: (product_rows(1, sub), 0)[1], 0)
        sum_products(1)
        send_back(1)

        for j in range(1, states):
            for t in range(per // 2):
                for h in range(2):
                    a_copy(h, j, t).wait_send()
                b_copy(j, t).wait_send()
            b_rest(j).wait_send()

        @pl.when(s == sweeps - 1)
        def _():
            def turn_u(t, _):
                for i in range(2):
                    u_ref[2 * t + i] = u_t[t, :, i * size : (i + 1) * size].T
                return 0

            lax.fori_loop(0, per // 2, turn_u, 0)

        for h in range(2):
            receive_back(h)

            @pl.when(s == sweeps - 1)
            def _():
                finish_all(h, True)

            @pl.when(s < sweeps - 1)
            def _():
                finish_all(h, False)
                send_near(h)
                send_far(h)

        return 0

    lax.fori_loop(0, sweeps, sweep, 0)


def per_device(kern_blocks, kern_cols, state_kernel, start_v, mu, nu):
    rows, degree, size, _ = kern_blocks.shape
    local_rows, cols = start_v.shape
    peers = lax.axis_size("mesh")
    states = lax.axis_size("state")
    me = lax.axis_index("mesh")
    per = rows // states
    nfar = (peers - 3) * FAR
    table_size = rows + 2 * NEAR + nfar
    nodes = states * cols
    dma = pltpu.SemaphoreType.DMA
    sources, requests = far_plan(kern_cols.reshape(-1), me, peers, rows)
    want = jnp.pad(requests, ((0, 0), (0, cols - FAR))).reshape(peers, 1, cols)
    pair_perm, pair_last = ordered_sums(sources, table_size)
    half = cols // 2

    def scratch(*dims, dtype=BF16):
        return pltpu.VMEM(dims + (half, size), dtype)

    potential_u, values = pl.pallas_call(
        functools.partial(solve_kernel, ITERS, peers, states),
        out_shape=(
            jax.ShapeDtypeStruct((per, size, nodes), F32),
            jax.ShapeDtypeStruct((rows, size, cols), F32),
        ),
        in_specs=[vmem()] + [smem()] * 3 + [hbm()] * 5,
        out_specs=(vmem(), vmem()),
        scratch_shapes=[
            pltpu.VMEM((rows, degree, size, size), BF16),
            pltpu.VMEM((nodes, nodes), BF16),
            pltpu.VMEM((nodes, nodes), BF16),
            pltpu.VMEM((per // 2, nodes, 2 * size), F32),
            pltpu.VMEM((rows, cols, size), F32),
            pltpu.VMEM((per // 2, nodes, 2 * size), F32),
            scratch(table_size),
            scratch(table_size),
            scratch(rows),
            scratch(rows),
            scratch(2, 2 * NEAR + nfar),
            scratch(rows * degree, dtype=F32),
            scratch(2, rows * degree),
            scratch(2 * NEAR + nfar),
            scratch(2 * NEAR + nfar),
            scratch(nfar, dtype=F32),
            pltpu.VMEM((peers - 1, 1, cols), jnp.int32),
            pltpu.VMEM((peers, cols), jnp.int32),
            pltpu.SMEM((peers - 1, 1, cols), jnp.int32),
            pltpu.SMEM((nfar,), jnp.int32),
            pltpu.SMEM((rows + 1,), jnp.int32),
            scratch(2, states, per),
            scratch(2, states, per),
            scratch(2, states, per),
            scratch(2, states, per),
            dma((7,)),
            dma((2, 2)), dma((2, 2)), dma((2,)), dma((2,)),
            dma((2, 2)), dma((2, 2)), dma((2,)), dma((2,)),
            dma((2, states, per // 2)), dma((2, states, per // 2)),
            dma((states, per // 2)), dma((states, per // 2)),
            dma((states,)), dma((states,)),
            dma((peers,)), dma,
        ],
        compiler_params=pltpu.CompilerParams(
            vmem_limit_bytes=VMEM_LIMIT, collective_id=0, has_side_effects=True
        ),
        name="solve",
    )(
        want, sources, pair_perm, pair_last,
        start_v.reshape(rows, size, cols), kern_blocks, state_kernel,
        mu.reshape(per, size, nodes),
        nu.reshape(rows, size, cols),
    )
    return (
        potential_u.reshape(local_rows // states, nodes),
        values.reshape(local_rows, cols),
    )


def solution(mesh):
    placed = (
        P("mesh", None, None, None),
        P("mesh", None),
        P(),
        P("mesh", "state"),
        P(("mesh", "state"), None),
        P("mesh", "state"),
    )
    return jax.shard_map(
        per_device,
        mesh=mesh,
        in_specs=placed,
        out_specs=(P(("mesh", "state"), None), P("mesh", "state")),
        check_vma=False,
    )
```
